32 devices in a mesh: groups: 2 (over x), space: 16 (over z, y, core).
Axes of the slice: x: 2, y: 2, z: 4, core: 2. Of those that a mesh axis runs over, the one named last changes fastest.
Arguments:
- eigvecs: bfloat16 [32, 64, 2, 3, 128], P('groups', 'space'), parts along dimension 0, may hold values from -1.3515625 to 1.3515625
- phase_index: int32 [128], P('groups'), parts along dimension 0, may hold values from 0 to 47
- perambulator: bfloat16 [512, 2, 128, 128], P(('groups', 'space')), parts along dimension 0, may hold values from -0.046875 to 0.046875
- tile_sink: int32 [512, 1], P(('groups', 'space')), parts along dimension 0, may hold values from 0 to 15; in each aligned block of 16 rows (0 to 15, 16 to 31, ...) at most 2 rows name the same one
- tile_sep: int32 [512], P(('groups', 'space')), parts along dimension 0, may hold values from 0 to 7
- tile_diagram: int32 [512], P(('groups', 'space')), parts along dimension 0, may hold values from 0 to 1
Outputs:
- elementals: bfloat16 [32, 2, 128, 128], P(('groups', 'space')), parts along dimension 0
- correlator: float32 [512, 2], P(('groups', 'space')), parts along dimension 0
The draws below stay inside these ranges and needn't reach their ends.
There are 2 independent parts, one for each index of `groups`. The reference program is written for one: setup_inputs(seed, part) draws one part's arguments, and reference() takes and returns one part's arrays. A program takes and returns all parts, laid end to end along the dimension named above; each array names one. Nothing has to cross between parts.
Inputs may be any that keep to these rules, and one draw needn't show every extreme that they name: `tile_sink`: in the tiles of one device no sink time is named by more than 2 tiles.
All inputs are finite; a program needn't handle non-finite values.
Results may differ from the reference program's by a relative error of at most 0.0048.
Values may be sent and summed in bfloat16 or wider, within the bound.
No kernel may reach another device: no remote copies, remote signals or barrier semaphores. Data moves between devices by JAX's collectives and lax.ppermute only.
A program may use at most 128 MiB of HBM per device.

```python
import math
import jax
import jax.numpy as jnp
import numpy as np
from jax import lax

NVEC = 128
COLORS = 3
PERIOD = 48
SEP = 8
CAP = 2
TIME = 16
SITES = 64
TILE_DEV = 16
TILES = 256


def with_ends(entries, stream_key, least, largest):
    longest = entries.shape.index(max(entries.shape))
    spots = []
    for shift in (0, 1):
        where = [jax.random.randint(jax.random.fold_in(stream_key, axis), (), 0, length) for axis, length in enumerate(entries.shape)]
        where[longest] = (where[longest] + shift) % entries.shape[longest]
        spots.append(tuple(where))
    return entries.at[spots[0]].set(least).at[spots[1]].set(largest)


def block_levels(rng, extent, split, low, top_value):
    gain = 1.0
    for dim, blocks in split:
        heights = jax.random.uniform(jax.random.fold_in(jax.random.fold_in(rng, 6), dim), (blocks,), jnp.float32, low / len(split), top_value / len(split))
        gain = gain * jnp.repeat(jnp.exp(heights), extent[dim] // blocks).reshape((-1,) + (1,) * (len(extent) - 1 - dim))
    return gain


def shared_out(rng, own, number, rows, count, top, limit, lean):
    sequence = jax.random.permutation(rng, count)
    crowded, ordinary = load_shares(count, rows * top, limit, lean, True), load_shares(count, rows * top, limit, lean, False)
    places = jnp.arange(count)

    def named(lengths, rotation):
        used = int((lengths > 0).sum())
        fixed = max(1, used // 4)
        moved = fixed + (places - fixed + rotation * (used - fixed)) % max(1, count - fixed)
        return jnp.zeros((count,), jnp.int32).at[sequence[jnp.where(places < fixed, places, moved)]].set(jnp.asarray(lengths, jnp.int32))

    lengths = jnp.where(number % 4 == 0, named(crowded, number // 4), named(ordinary, number - number // 4 - 1))
    mixed = jax.random.permutation(jax.random.fold_in(own, 3), count)
    donor, taker = mixed[0:count // 2 * 2:2], mixed[1:count // 2 * 2:2]
    slack = jnp.minimum(lengths[donor] - 1, limit - lengths[taker]) // 2
    slack = jnp.where((donor == sequence[0]) | (taker == sequence[0]) | (lengths[taker] == 0), 0, jnp.maximum(slack, 0))
    moved = jax.random.randint(jax.random.fold_in(own, 4), (count // 2,), 0, 1 << 20) % (slack + 1)
    lengths = lengths.at[donor].add(-moved).at[taker].add(moved)
    labels = jnp.searchsorted(jnp.cumsum(lengths), jnp.arange(rows * top), side="right").astype(jnp.int32)
    grid = labels.reshape(top, rows).T
    grid = grid[jax.random.permutation(jax.random.fold_in(own, 1), rows)]
    rotation = jax.random.randint(jax.random.fold_in(own, 2), (rows, 1), 0, top)
    return jnp.take_along_axis(grid, (jnp.arange(top)[None, :] + rotation) % top, axis=1)


def load_shares(count, total, bound, lean, full):
    loads = [(1 << 20) // math.isqrt(standing ** lean) + 1 for standing in range(1, count + 1)]
    largest = bound if full else min(bound, max(-(-total // count), total * loads[0] // sum(loads)))
    least = 1 if total - largest >= count - 1 else 0
    holding, rest = [largest] + [least] * (count - 1), total - largest - least * (count - 1)
    while rest > 0:
        free = [i for i in range(1, count) if holding[i] < largest] or [i for i in range(1, count) if holding[i] < bound]
        mass, remaining = sum([loads[i] for i in free]), rest
        for i in free:
            addition = min(bound - holding[i], max(1, remaining * loads[i] // mass), rest)
            holding[i] = holding[i] + addition
            rest = rest - addition
    return np.array(holding)


def normal_values(own_key, shape, deviation, most, cuts=(), held_as=jnp.bfloat16):
    array = deviation * jax.random.normal(own_key, shape, jnp.float32)
    if cuts:
        array = array * block_levels(own_key, shape, cuts, -0.22, 0.18)
    return jnp.clip(array, -most, most).astype(held_as)


def setup_inputs(seed: int = 0, part: int = 0) -> dict:
    streams_of = jax.random.split(jax.random.key(seed), 7)
    own_keys = jax.random.split(jax.random.fold_in(streams_of[6], part), 7)
    eigvecs = normal_values(own_keys[0], (TIME, SITES, 2, COLORS, NVEC), (1.0 / (6 * SITES) ** 0.25), 1.3515625, ((1, 16),))
    phase_index = with_ends(jax.random.randint(own_keys[1], (SITES,), 0, PERIOD), jax.random.fold_in(own_keys[1], 1), 0, PERIOD - 1).astype(jnp.int32)
    perambulator = normal_values(own_keys[2], (TILES, 2, NVEC, NVEC), 0.0078125, 0.046875, ((0, 16),))
    tile_sink_keys = jax.random.split(jax.random.fold_in(own_keys[3], 1), TILES // TILE_DEV)
    tile_sink_turns = jax.random.permutation(jax.random.fold_in(own_keys[3], 3), TILES // TILE_DEV)
    tile_sink = jax.vmap(lambda own, number: shared_out(jax.random.fold_in(own_keys[3], 2), own, number, TILE_DEV, TIME, 1, CAP, 2))(tile_sink_keys, tile_sink_turns).reshape((TILES, 1))
    tile_sep = with_ends(jax.random.randint(own_keys[4], (TILES,), 0, SEP), jax.random.fold_in(own_keys[4], 1), 0, SEP - 1).astype(jnp.int32)
    tile_diagram = with_ends(jax.random.randint(own_keys[5], (TILES,), 0, 2), jax.random.fold_in(own_keys[5], 1), 0, 1).astype(jnp.int32)
    return dict(eigvecs=eigvecs, phase_index=phase_index, perambulator=perambulator, tile_sink=tile_sink, tile_sep=tile_sep, tile_diagram=tile_diagram)


def make_right(vecs, cosine, sine):
    real_part = vecs[..., 0, :, :].astype(jnp.float32)
    imag_part = vecs[..., 1, :, :].astype(jnp.float32)
    cos_col = cosine[:, None, None]
    sin_col = sine[:, None, None]
    first = (cos_col * real_part - sin_col * imag_part).astype(jnp.bfloat16)
    second = (sin_col * real_part + cos_col * imag_part).astype(jnp.bfloat16)
    top = jnp.stack([first, second], -2)
    bottom = jnp.stack([second, -first], -2)
    return jnp.stack([top, bottom], -4)


def contract_tiles(sink_mat, source_mat, tiles, diagram):
    def mult(left, right):
        return jnp.einsum("bij,bjk->bik", left.astype(jnp.float32), right.astype(jnp.float32))

    tile_re = tiles[:, 0]
    tile_im = tiles[:, 1]
    trans_re = jnp.swapaxes(tile_re, 1, 2)
    trans_im = -jnp.swapaxes(tile_im, 1, 2)
    flag = (diagram == 1)[:, None, None]
    left_re = jnp.where(flag, trans_re, tile_re)
    left_im = jnp.where(flag, trans_im, tile_im)
    right_re = jnp.where(flag, tile_re, trans_re)
    right_im = jnp.where(flag, tile_im, trans_im)
    sink_re = sink_mat[:, 0]
    sink_im = sink_mat[:, 1]
    src_re = jnp.swapaxes(source_mat[:, 0], 1, 2)
    src_im = -jnp.swapaxes(source_mat[:, 1], 1, 2)
    first_re = mult(sink_re, left_re) - mult(sink_im, left_im)
    first_im = mult(sink_re, left_im) + mult(sink_im, left_re)
    second_re = mult(src_re, right_re) - mult(src_im, right_im)
    second_im = mult(src_re, right_im) + mult(src_im, right_re)
    second_re = jnp.swapaxes(second_re, 1, 2)
    second_im = jnp.swapaxes(second_im, 1, 2)
    trace_re = jnp.sum(first_re * second_re - first_im * second_im, axis=(1, 2))
    trace_im = jnp.sum(first_re * second_im + first_im * second_re, axis=(1, 2))
    return jnp.stack([trace_re, trace_im], -1)


def reference(eigvecs, phase_index, perambulator, tile_sink, tile_sep, tile_diagram):
    angle = (2.0 * math.pi / PERIOD) * phase_index.astype(jnp.float32)
    cosine = jnp.cos(angle)
    sine = jnp.sin(angle)

    def one_slice(vecs):
        right = make_right(vecs, cosine, sine)
        value = jnp.einsum("spck,spcol->okl", vecs.astype(jnp.float32), right.astype(jnp.float32))
        return value.astype(jnp.bfloat16)

    elementals = lax.map(one_slice, eigvecs)
    total = perambulator.shape[0]
    block = math.gcd(32, total)
    sinks = tile_sink[:, 0].astype(jnp.int32)
    sources = jnp.mod(sinks - tile_sep, TIME).astype(jnp.int32)

    def one_block(items):
        tiles, sink_ids, source_ids, diagram = items
        return contract_tiles(elementals[sink_ids], elementals[source_ids], tiles, diagram)

    shaped = (perambulator.reshape((total // block, block) + perambulator.shape[1:]),
              sinks.reshape(total // block, block), sources.reshape(total // block, block),
              tile_diagram.reshape(total // block, block))
    correlator = lax.map(one_block, shaped).reshape(total, 2)
    return elementals, correlator
```

```python
import functools
import math

import jax
import jax.numpy as jnp
from jax import lax
from jax.experimental import pallas as pl
from jax.experimental.pallas import tpu as pltpu
from jax.sharding import PartitionSpec as P

PERIOD = 48
AXIS = "space"
GATHER_BYTES = 8 << 20
VMEM_LIMIT = 48 << 20


def phases(indices):
    angle = 2.0 * math.pi / PERIOD * indices.astype(jnp.float32)
    return (jnp.cos(angle), jnp.sin(angle))


def swap(block, offset):
    size = lax.axis_size(AXIS)
    return lax.ppermute(block, AXIS, [(i, i ^ offset) for i in range(size)])


def exchange(block):
    held = {0: block}
    bit = lax.axis_size(AXIS) // 2
    while bit >= 8:
        held.update({k ^ bit: swap(b, bit) for k, b in list(held.items())})
        bit //= 2
    for stage in ((4, 2, 6), (1,)):
        fresh = {}
        for step in stage:
            if step < lax.axis_size(AXIS):
                fresh.update({k ^ step: swap(b, step) for k, b in held.items()})
        held.update(fresh)
    return held


def rotated(vecs, cosine, sine):
    rows = vecs.shape[0]
    groups = vecs.reshape(rows // 8, 8, vecs.shape[1])
    even = lax.broadcasted_iota(jnp.int32, groups.shape, 1) % 2 == 0
    turned = jnp.where(even, -pltpu.roll(groups, 7, 1), pltpu.roll(groups, 1, 1)).reshape(vecs.shape)
    first = cosine * vecs + sine * turned
    second = sine * vecs - cosine * turned
    return first.astype(jnp.bfloat16), second.astype(jnp.bfloat16)


def tile_terms(left, right, left_turned, right_turned, tile_re, tile_im):
    n = tile_re.shape[0]
    dot = functools.partial(jnp.dot, preferred_element_type=jnp.float32)
    tile = jnp.concatenate([tile_re, tile_im], 1)
    turned = jnp.concatenate([-tile_im, tile_re], 1)
    first = dot(left, jnp.concatenate([tile, turned], 0))
    second = dot(tile, jnp.concatenate([right, right_turned], 0))
    fr, fi, sr, si = first[:, :n], first[:, n:], second[:, :n], second[:, n:]
    return (
        jnp.sum(fr * sr + fi * si, axis=0, keepdims=True),
        jnp.sum(fi * sr - fr * si, axis=0, keepdims=True),
    )


def contract(left_ref, right_ref, sign_ref, plain, turned, tiles_ref, re_ref, im_ref, corr_ref):
    count = tiles_ref.shape[0]

    def step(i, carry):
        a, b = left_ref[i], right_ref[i]
        re, im = tile_terms(plain[a], plain[b], turned[a], turned[b], tiles_ref[i, 0], tiles_ref[i, 1])
        re_ref[pl.ds(i, 1), :] = re
        im_ref[pl.ds(i, 1), :] = im * sign_ref[i].astype(jnp.float32)
        return carry

    lax.fori_loop(0, count, step, 0, unroll=4)
    corr_ref[...] = jnp.concatenate(
        [jnp.sum(re_ref[...], axis=1, keepdims=True), jnp.sum(im_ref[...], axis=1, keepdims=True)], 1
    )


def fused_kernel(offsets, left_ref, right_ref, sign_ref, me_ref, cos_ref, sin_ref, tiles_ref, *refs):
    blocks = refs[: len(offsets)]
    own_ref, corr_ref, plain, turned, re_ref, im_ref = refs[len(offsets):]
    times, n = blocks[0].shape[0], blocks[0].shape[2]
    me = me_ref[0]
    cosine = jnp.concatenate([cos_ref[me ^ k] for k in offsets], 0)
    sine = jnp.concatenate([sin_ref[me ^ k] for k in offsets], 0)

    def slice_step(t, carry):
        vecs = jnp.concatenate([b[t].astype(jnp.float32) for b in blocks], 0)
        first, second = rotated(vecs, cosine, sine)
        value = lax.dot_general(
            vecs.astype(jnp.bfloat16),
            jnp.concatenate([first, second], 1),
            (((0,), (0,)), ((), ())),
            preferred_element_type=jnp.float32,
        ).astype(jnp.bfloat16)
        plain[t] = value
        turned[t] = jnp.concatenate([-value[:, n:], value[:, :n]], 1)
        return carry

    lax.fori_loop(0, times, slice_step, 0, unroll=2)
    own = plain[me]
    own_ref[0, 0] = own[:, :n]
    own_ref[0, 1] = own[:, n:]
    contract(left_ref, right_ref, sign_ref, plain, turned, tiles_ref, re_ref, im_ref, corr_ref)


def tile_operands(tile_sink, tile_sep, tile_diagram, times):
    sinks = tile_sink[:, 0]
    sources = jnp.mod(sinks - tile_sep, times)
    flipped = tile_diagram == 1
    left = jnp.where(flipped, sources, sinks).astype(jnp.int32)
    right = jnp.where(flipped, sinks, sources).astype(jnp.int32)
    sign = jnp.where(flipped, -1, 1).astype(jnp.int32)
    return left, right, sign


def by_gathered_vectors(eigvecs, phase_index, perambulator, tile_sink, tile_sep, tile_diagram):
    times, sites, parts, colors, n = eigvecs.shape
    devices = lax.axis_size(AXIS)
    rows = sites * colors * parts
    block = eigvecs.transpose(0, 1, 3, 2, 4).reshape(times, rows, n)
    held = exchange(block)
    offsets = tuple(sorted(held))
    cosine, sine = phases(phase_index)

    def spread(column):
        return jnp.broadcast_to(column.reshape(devices, sites, 1, 1), (devices, sites, colors * parts, n)).reshape(devices, rows, n)

    left, right, sign = tile_operands(tile_sink, tile_sep, tile_diagram, times)
    me = lax.axis_index(AXIS).astype(jnp.int32)[None]
    tiles = perambulator.shape[0]
    smem = pl.BlockSpec(memory_space=pltpu.SMEM)
    vmem = pl.BlockSpec(memory_space=pltpu.VMEM)
    return pl.pallas_call(
        functools.partial(fused_kernel, offsets),
        out_shape=(
            jax.ShapeDtypeStruct((1, 2, n, n), jnp.bfloat16),
            jax.ShapeDtypeStruct((tiles, 2), jnp.float32),
        ),
        in_specs=[smem] * 4 + [vmem] * (3 + len(offsets)),
        out_specs=(vmem, vmem),
        scratch_shapes=[
            pltpu.VMEM((times, n, 2 * n), jnp.bfloat16),
            pltpu.VMEM((times, n, 2 * n), jnp.bfloat16),
            pltpu.VMEM((tiles, n), jnp.float32),
            pltpu.VMEM((tiles, n), jnp.float32),
        ],
        compiler_params=pltpu.CompilerParams(vmem_limit_bytes=VMEM_LIMIT),
    )(left, right, sign, me, spread(cosine), spread(sine), perambulator, *[held[k] for k in offsets])


def contract_kernel(left_ref, right_ref, sign_ref, elementals_ref, tiles_ref, corr_ref, plain, turned, re_ref, im_ref):
    times = elementals_ref.shape[0]

    def widen(t, carry):
        re, im = elementals_ref[t, 0], elementals_ref[t, 1]
        plain[t] = jnp.concatenate([re, im], 1)
        turned[t] = jnp.concatenate([-im, re], 1)
        return carry

    lax.fori_loop(0, times, widen, 0)
    contract(left_ref, right_ref, sign_ref, plain, turned, tiles_ref, re_ref, im_ref, corr_ref)


def by_gathered_elementals(eigvecs, phase_index, perambulator, tile_sink, tile_sep, tile_diagram):
    cosine, sine = phases(phase_index)
    vecs = lax.all_to_all(eigvecs, AXIS, split_axis=0, concat_axis=1, tiled=True)[0].astype(jnp.float32)
    cosine, sine = cosine[:, None, None], sine[:, None, None]
    first = cosine * vecs[:, 0] - sine * vecs[:, 1]
    second = sine * vecs[:, 0] + cosine * vecs[:, 1]
    right = jnp.stack([jnp.stack([first, second], -2), jnp.stack([second, -first], -2)], -4).astype(jnp.bfloat16)
    value = jnp.einsum("spck,spcol->okl", vecs.astype(jnp.bfloat16), right, preferred_element_type=jnp.float32)
    elemental = value.astype(jnp.bfloat16)[None]
    gathered = lax.all_gather(elemental, AXIS, axis=0, tiled=True)
    times, _, n, _ = gathered.shape
    tiles = perambulator.shape[0]
    left, right, sign = tile_operands(tile_sink, tile_sep, tile_diagram, times)
    smem = pl.BlockSpec(memory_space=pltpu.SMEM)
    vmem = pl.BlockSpec(memory_space=pltpu.VMEM)
    correlator = pl.pallas_call(
        contract_kernel,
        out_shape=jax.ShapeDtypeStruct((tiles, 2), jnp.float32),
        in_specs=[smem] * 3 + [vmem] * 2,
        out_specs=vmem,
        scratch_shapes=[
            pltpu.VMEM((times, n, 2 * n), jnp.bfloat16),
            pltpu.VMEM((times, n, 2 * n), jnp.bfloat16),
            pltpu.VMEM((tiles, n), jnp.float32),
            pltpu.VMEM((tiles, n), jnp.float32),
        ],
        compiler_params=pltpu.CompilerParams(vmem_limit_bytes=VMEM_LIMIT),
    )(left, right, sign, gathered, perambulator)
    return elemental, correlator


def local(eigvecs, *rest):
    devices = lax.axis_size(AXIS)
    small = eigvecs.size * eigvecs.dtype.itemsize * devices <= GATHER_BYTES
    if small and devices & (devices - 1) == 0:
        return by_gathered_vectors(eigvecs, *rest)
    return by_gathered_elementals(eigvecs, *rest)


def solution(mesh):
    return jax.shard_map(
        local,
        mesh=mesh,
        in_specs=(
            P("groups", "space", None, None, None),
            P("groups"),
            P(("groups", "space"), None, None, None),
            P(("groups", "space"), None),
            P(("groups", "space")),
            P(("groups", "space")),
        ),
        out_specs=(P(("groups", "space"), None, None, None), P(("groups", "space"), None)),
        check_vma=False,
    )
```

```python
import functools
import math

import jax
import jax.numpy as jnp
from jax import lax
from jax.experimental import pallas as pl
from jax.experimental.pallas import tpu as pltpu
from jax.sharding import PartitionSpec as P

PERIOD = 48
AXIS = "space"
GATHER_BYTES = 8 << 20
VMEM_LIMIT = 48 << 20


def phases(indices):
    angle = 2.0 * math.pi / PERIOD * indices.astype(jnp.float32)
    return (jnp.cos(angle), jnp.sin(angle))


def swap(block, offset):
    size = lax.axis_size(AXIS)
    return lax.ppermute(block, AXIS, [(i, i ^ offset) for i in range(size)])


def exchange(block):
    held = {0: block}
    bit = lax.axis_size(AXIS) // 2
    while bit >= 8:
        held.update({k ^ bit: swap(b, bit) for k, b in list(held.items())})
        bit //= 2
    for stage in ((4, 2, 6), (1,)):
        fresh = {}
        for step in stage:
            if step < lax.axis_size(AXIS):
                fresh.update({k ^ step: swap(b, step) for k, b in held.items()})
        held.update(fresh)
    return held


def swapped(values):
    other = lax.broadcasted_iota(jnp.int32, (8, values.shape[1]), 0) ^ 1
    pieces = [jnp.take_along_axis(values[i : i + 8], other, axis=0) for i in range(0, values.shape[0], 8)]
    return jnp.concatenate(pieces, 0)


def tile_terms(left, right, left_turned, right_turned, tile):
    n = tile.shape[0]
    dot = functools.partial(jnp.dot, preferred_element_type=jnp.float32)
    turned = jnp.concatenate([-tile[:, n:], tile[:, :n]], 1)
    first = dot(left, jnp.concatenate([tile, turned], 0))
    second = dot(tile, jnp.concatenate([right, right_turned], 0))
    fr, fi, sr, si = first[:, :n], first[:, n:], second[:, :n], second[:, n:]
    return (
        jnp.sum(fr * sr + fi * si, axis=0, keepdims=True),
        jnp.sum(fi * sr - fr * si, axis=0, keepdims=True),
    )


def contract(left_ref, right_ref, sign_ref, plain, turned, tiles_ref, re_ref, im_ref, corr_ref):
    count = tiles_ref.shape[0]

    def step(i, carry):
        a, b = left_ref[i], right_ref[i]
        re, im = tile_terms(plain[a], plain[b], turned[a], turned[b], tiles_ref[i])
        re_ref[pl.ds(i, 1), :] = re
        im_ref[pl.ds(i, 1), :] = im * sign_ref[i].astype(jnp.float32)
        return carry

    lax.fori_loop(0, count, step, 0, unroll=math.gcd(count, 16))
    corr_ref[0, :] = jnp.sum(re_ref[...], axis=1)
    corr_ref[1, :] = jnp.sum(im_ref[...], axis=1)


def fill_tables(blocks, rows, sites, owner, cos_ref, sin_ref, tables):
    n = tables[0].shape[1]
    row = lax.broadcasted_iota(jnp.int32, (rows, n), 0)
    sign = jnp.where(row % 2 == 0, -1.0, 1.0)
    for j in range(blocks):
        first = owner(j) * sites
        for source, plain, signed in ((cos_ref, tables[0], tables[2]), (sin_ref, tables[1], tables[3])):
            value = jnp.full((rows, n), source[first], jnp.float32)
            for q in range(1, sites):
                value = jnp.where(row >= q * (rows // sites), source[first + q], value)
            plain[pl.ds(j * rows, rows)] = value
            signed[pl.ds(j * rows, rows)] = value * sign


def fused_kernel(offsets, sites, left_ref, right_ref, sign_ref, me_ref, cos_ref, sin_ref, tiles_ref, own_hbm, *refs):
    received = refs[: len(offsets) - 1]
    own_ref, corr_ref, plain, turned, re_ref, im_ref, block_ref, sems, *tables = refs[len(offsets) - 1 :]
    load_block = pltpu.make_async_copy(own_hbm, block_ref, sems.at[0])
    load_block.start()
    times, rows, n = block_ref.shape
    me = me_ref[0]
    fill_tables(len(offsets), rows, sites, lambda j: me ^ offsets[j], cos_ref, sin_ref, tables)
    cosine, sine, cosine_signed, sine_signed = tables
    load_block.wait()
    blocks = (block_ref, *received)

    def slice_step(t, carry):
        vecs = jnp.concatenate([b[t].astype(jnp.float32) for b in blocks], 0)
        other = swapped(vecs)
        first = cosine[...] * vecs + sine_signed[...] * other
        second = sine[...] * vecs - cosine_signed[...] * other
        value = lax.dot_general(
            vecs.astype(jnp.bfloat16),
            jnp.concatenate([first.astype(jnp.bfloat16), second.astype(jnp.bfloat16)], 1),
            (((0,), (0,)), ((), ())),
            preferred_element_type=jnp.float32,
        ).astype(jnp.bfloat16)
        plain[t] = value
        turned[t] = jnp.concatenate([-value[:, n:], value[:, :n]], 1)
        return carry

    lax.fori_loop(0, times, slice_step, 0, unroll=True)
    own = plain[me]
    own_ref[0, 0] = own[:, :n]
    own_ref[0, 1] = own[:, n:]
    contract(left_ref, right_ref, sign_ref, plain, turned, tiles_ref, re_ref, im_ref, corr_ref)


def widened(perambulator):
    return jnp.concatenate([perambulator[:, 0], perambulator[:, 1]], 2)


def tile_operands(tile_sink, tile_sep, tile_diagram, times):
    sinks = tile_sink[:, 0]
    sources = jnp.mod(sinks - tile_sep, times)
    flipped = tile_diagram == 1
    left = jnp.where(flipped, sources, sinks).astype(jnp.int32)
    right = jnp.where(flipped, sinks, sources).astype(jnp.int32)
    sign = jnp.where(flipped, -1, 1).astype(jnp.int32)
    return left, right, sign


def by_gathered_vectors(eigvecs, phase_index, perambulator, tile_sink, tile_sep, tile_diagram):
    times, sites, parts, colors, n = eigvecs.shape
    devices = lax.axis_size(AXIS)
    rows = sites * colors * parts
    block = eigvecs.transpose(0, 1, 3, 2, 4).reshape(times, rows, n)
    held = exchange(block)
    offsets = (0, *sorted(held, reverse=True)[:-1])
    cosine, sine = phases(phase_index)
    left, right, sign = tile_operands(tile_sink, tile_sep, tile_diagram, times)
    me = lax.axis_index(AXIS).astype(jnp.int32)[None]
    tiles = perambulator.shape[0]
    wide = widened(perambulator)
    smem = pl.BlockSpec(memory_space=pltpu.SMEM)
    vmem = pl.BlockSpec(memory_space=pltpu.VMEM)
    hbm = pl.BlockSpec(memory_space=pltpu.HBM)
    elemental, correlator = pl.pallas_call(
        functools.partial(fused_kernel, offsets, sites),
        out_shape=(
            jax.ShapeDtypeStruct((1, 2, n, n), jnp.bfloat16),
            jax.ShapeDtypeStruct((2, tiles), jnp.float32),
        ),
        in_specs=[smem] * 6 + [vmem, hbm] + [vmem] * (devices - 1),
        out_specs=(vmem, vmem),
        scratch_shapes=[
            pltpu.VMEM((times, n, 2 * n), jnp.bfloat16),
            pltpu.VMEM((times, n, 2 * n), jnp.bfloat16),
            pltpu.VMEM((tiles, n), jnp.float32),
            pltpu.VMEM((tiles, n), jnp.float32),
            pltpu.VMEM(block.shape, block.dtype),
            pltpu.SemaphoreType.DMA((2,)),
        ]
        + [pltpu.VMEM((devices * rows, n), jnp.float32)] * 4,
        compiler_params=pltpu.CompilerParams(vmem_limit_bytes=VMEM_LIMIT),
    )(left, right, sign, me, cosine, sine, wide, block, *[held[k] for k in offsets[1:]])
    return elemental, correlator.T


def contract_kernel(left_ref, right_ref, sign_ref, elementals_ref, tiles_ref, corr_ref, plain, turned, re_ref, im_ref):
    times = elementals_ref.shape[0]

    def widen(t, carry):
        re, im = elementals_ref[t, 0], elementals_ref[t, 1]
        plain[t] = jnp.concatenate([re, im], 1)
        turned[t] = jnp.concatenate([-im, re], 1)
        return carry

    lax.fori_loop(0, times, widen, 0)
    contract(left_ref, right_ref, sign_ref, plain, turned, tiles_ref, re_ref, im_ref, corr_ref)


def by_gathered_elementals(eigvecs, phase_index, perambulator, tile_sink, tile_sep, tile_diagram):
    cosine, sine = phases(phase_index)
    vecs = lax.all_to_all(eigvecs, AXIS, split_axis=0, concat_axis=1, tiled=True)[0].astype(jnp.float32)
    cosine, sine = cosine[:, None, None], sine[:, None, None]
    first = cosine * vecs[:, 0] - sine * vecs[:, 1]
    second = sine * vecs[:, 0] + cosine * vecs[:, 1]
    right = jnp.stack([jnp.stack([first, second], -2), jnp.stack([second, -first], -2)], -4).astype(jnp.bfloat16)
    value = jnp.einsum("spck,spcol->okl", vecs.astype(jnp.bfloat16), right, preferred_element_type=jnp.float32)
    elemental = value.astype(jnp.bfloat16)[None]
    gathered = lax.all_gather(elemental, AXIS, axis=0, tiled=True)
    times, _, n, _ = gathered.shape
    tiles = perambulator.shape[0]
    left, right, sign = tile_operands(tile_sink, tile_sep, tile_diagram, times)
    smem = pl.BlockSpec(memory_space=pltpu.SMEM)
    vmem = pl.BlockSpec(memory_space=pltpu.VMEM)
    correlator = pl.pallas_call(
        contract_kernel,
        out_shape=jax.ShapeDtypeStruct((2, tiles), jnp.float32),
        in_specs=[smem] * 3 + [vmem] * 2,
        out_specs=vmem,
        scratch_shapes=[
            pltpu.VMEM((times, n, 2 * n), jnp.bfloat16),
            pltpu.VMEM((times, n, 2 * n), jnp.bfloat16),
            pltpu.VMEM((tiles, n), jnp.float32),
            pltpu.VMEM((tiles, n), jnp.float32),
        ],
        compiler_params=pltpu.CompilerParams(vmem_limit_bytes=VMEM_LIMIT),
    )(left, right, sign, gathered, widened(perambulator))
    return elemental, correlator.T


def local(eigvecs, *rest):
    devices = lax.axis_size(AXIS)
    small = eigvecs.size * eigvecs.dtype.itemsize * devices <= GATHER_BYTES
    if small and devices & (devices - 1) == 0:
        return by_gathered_vectors(eigvecs, *rest)
    return by_gathered_elementals(eigvecs, *rest)


def solution(mesh):
    return jax.shard_map(
        local,
        mesh=mesh,
        in_specs=(
            P("groups", "space", None, None, None),
            P("groups"),
            P(("groups", "space"), None, None, None),
            P(("groups", "space"), None),
            P(("groups", "space")),
            P(("groups", "space")),
        ),
        out_specs=(P(("groups", "space"), None, None, None), P(("groups", "space"), None)),
        check_vma=False,
    )
```

```python
import functools
import math

import jax
import jax.numpy as jnp
from jax import lax
from jax.experimental import pallas as pl
from jax.experimental.pallas import tpu as pltpu
from jax.sharding import PartitionSpec as P

PERIOD = 48
AXIS = "space"
GATHER_BYTES = 8 << 20
VMEM_LIMIT = 48 << 20


def phases(indices):
    angle = 2.0 * math.pi / PERIOD * indices.astype(jnp.float32)
    return (jnp.cos(angle), jnp.sin(angle))


def swap(block, offset):
    size = lax.axis_size(AXIS)
    return lax.ppermute(block, AXIS, [(i, i ^ offset) for i in range(size)])


def step(held, offset):
    return [(swap(array, offset), tuple(k ^ offset for k in owners)) for array, owners in held]


def stacked(held):
    return jnp.stack([array for array, _ in held], 0), sum((owners for _, owners in held), ())


def swapped(values):
    other = lax.broadcasted_iota(jnp.int32, (8, values.shape[1]), 0) ^ 1
    pieces = [jnp.take_along_axis(values[i : i + 8], other, axis=0) for i in range(0, values.shape[0], 8)]
    return jnp.concatenate(pieces, 0)


def tile_terms(left, right, left_turned, right_turned, tile):
    n = tile.shape[0]
    dot = functools.partial(jnp.dot, preferred_element_type=jnp.float32)
    turned = jnp.concatenate([-tile[:, n:], tile[:, :n]], 1)
    first = dot(left, jnp.concatenate([tile, turned], 0))
    second = dot(tile, jnp.concatenate([right, right_turned], 0))
    fr, fi, sr, si = first[:, :n], first[:, n:], second[:, :n], second[:, n:]
    return (
        jnp.sum(fr * sr + fi * si, axis=0, keepdims=True),
        jnp.sum(fi * sr - fr * si, axis=0, keepdims=True),
    )


def pick(sink_ref, sep_ref, diagram_ref, i, times):
    sink = sink_ref[i]
    source = lax.rem(lax.rem(sink - sep_ref[i], times) + times, times)
    flipped = diagram_ref[i] == 1
    return jnp.where(flipped, source, sink), jnp.where(flipped, sink, source), jnp.where(flipped, -1.0, 1.0)


def contract(ids, plain, turned, tiles_ref, re_ref, im_ref, corr_ref):
    count = tiles_ref.shape[0]

    def one(i, carry):
        a, b, sign = pick(*ids, i, plain.shape[0])
        re, im = tile_terms(plain[a], plain[b], turned[a], turned[b], tiles_ref[i])
        re_ref[pl.ds(i, 1), :] = re
        im_ref[pl.ds(i, 1), :] = im * sign
        return carry

    lax.fori_loop(0, count, one, 0, unroll=math.gcd(count, 16))
    corr_ref[0, :] = jnp.sum(re_ref[...], axis=1)
    corr_ref[1, :] = jnp.sum(im_ref[...], axis=1)


def block_list(refs, pieces):
    loads, owners = [], []
    for ref, piece in zip(refs, pieces):
        for i, k in enumerate(piece):
            loads.append(functools.partial(lambda r, t: r[t], ref if len(piece) == 1 else ref.at[i]))
            owners.append(k)
    return loads, owners


def fill_tables(owners, rows, me, phase_refs, tables):
    n, sites = tables[0].shape[-1], phase_refs[0].shape[1]
    row = lax.broadcasted_iota(jnp.int32, (rows, n), 0)
    sign = jnp.where(row % 2 == 0, -1.0, 1.0)
    for j, k in enumerate(owners):
        for source, plain, signed in zip(phase_refs, tables[:2], tables[2:]):
            line = source[pl.ds(me ^ k, 1), :]
            value = jnp.broadcast_to(line[:, :1], (rows, n))
            for q in range(1, sites):
                value = jnp.where(row >= q * (rows // sites), jnp.broadcast_to(line[:, q : q + 1], (rows, n)), value)
            plain[pl.ds(j * rows, rows)] = value
            signed[pl.ds(j * rows, rows)] = value * sign


def slice_values(loads, t, tables):
    cosine, sine, cosine_signed, sine_signed = tables
    vecs = jnp.concatenate([load(t).astype(jnp.float32) for load in loads], 0)
    other = swapped(vecs)
    first = cosine[...] * vecs + sine_signed[...] * other
    second = sine[...] * vecs - cosine_signed[...] * other
    return lax.dot_general(
        vecs.astype(jnp.bfloat16),
        jnp.concatenate([first.astype(jnp.bfloat16), second.astype(jnp.bfloat16)], 1),
        (((0,), (0,)), ((), ())),
        preferred_element_type=jnp.float32,
    )


def fused_kernel(pieces, cos_ref, sin_ref, sink_any, sep_any, diagram_any, own_any, tiles_ref, *refs):
    held = refs[: len(pieces)]
    elemental_any, corr_ref, plain, turned, re_ref, im_ref, block_ref, out_ref, *rest = refs[len(pieces) :]
    ids, sems, tables = rest[:3], rest[3], rest[4:]
    loads_in = [
        pltpu.make_async_copy(source, target, sems.at[i])
        for i, (source, target) in enumerate(zip((own_any, sink_any, sep_any, diagram_any), (block_ref, *ids)))
    ]
    for load in loads_in:
        load.start()
    loads, owners = block_list((block_ref, *held), ((0,), *pieces))
    times, rows, n = block_ref.shape
    me = lax.axis_index(AXIS).astype(jnp.int32)
    fill_tables(owners, rows, me, (cos_ref, sin_ref), tables)
    loads_in[0].wait()
    for t in range(times):
        value = slice_values(loads, t, tables).astype(jnp.bfloat16)
        plain[t] = value
        turned[t] = jnp.concatenate([-value[:, n:], value[:, :n]], 1)
    own = plain[me]
    out_ref[0, 0] = own[:, :n]
    out_ref[0, 1] = own[:, n:]
    store = pltpu.make_async_copy(out_ref, elemental_any, sems.at[4])
    store.start()
    for load in loads_in[1:]:
        load.wait()
    contract(ids, plain, turned, tiles_ref, re_ref, im_ref, corr_ref)
    store.wait()


def widened(perambulator):
    return jnp.concatenate([perambulator[:, 0], perambulator[:, 1]], 2)


def by_gathered_vectors(eigvecs, phase_index, perambulator, tile_sink, tile_sep, tile_diagram):
    times, sites, parts, colors, n = eigvecs.shape
    devices = lax.axis_size(AXIS)
    rows = sites * colors * parts
    block = eigvecs.transpose(0, 1, 3, 2, 4).reshape(times, rows, n)
    own = (block, (0,))
    [far] = step([own], 8)
    [d], [b], [y] = step([own], 6), step([own], 4), step([own], 2)
    [fd], [fb], [fy] = step([far], 6), step([far], 4), step([far], 2)
    near = stacked([far, d, b, y])
    so, sn = step([own, near], 1)
    rest = stacked([fd, fb, fy])
    [sr] = step([rest], 1)
    held = [rest, sn, sr, far, d, b, y, so]
    cosine, sine = (value.reshape(devices, sites) for value in phases(phase_index))
    tiles = perambulator.shape[0]
    vmem = pl.BlockSpec(memory_space=pltpu.VMEM)
    anywhere = pl.BlockSpec(memory_space=pl.ANY)
    elemental, correlator = pl.pallas_call(
        functools.partial(fused_kernel, [owners for _, owners in held]),
        out_shape=(
            jax.ShapeDtypeStruct((1, 2, n, n), jnp.bfloat16),
            jax.ShapeDtypeStruct((2, tiles), jnp.float32),
        ),
        in_specs=[vmem] * 2 + [anywhere] * 4 + [vmem] * (1 + len(held)),
        out_specs=(anywhere, vmem),
        scratch_shapes=[
            pltpu.VMEM((times, n, 2 * n), jnp.bfloat16),
            pltpu.VMEM((times, n, 2 * n), jnp.bfloat16),
            pltpu.VMEM((tiles, n), jnp.float32),
            pltpu.VMEM((tiles, n), jnp.float32),
            pltpu.VMEM(block.shape, block.dtype),
            pltpu.VMEM((1, 2, n, n), jnp.bfloat16),
            *[pltpu.SMEM((tiles,), jnp.int32)] * 3,
            pltpu.SemaphoreType.DMA((5,)),
        ]
        + [pltpu.VMEM((devices * rows, n), jnp.float32)] * 4,
        compiler_params=pltpu.CompilerParams(vmem_limit_bytes=VMEM_LIMIT),
    )(cosine, sine, tile_sink[:, 0], tile_sep, tile_diagram, block, widened(perambulator), *[array for array, _ in held])
    return elemental, correlator.T


def contract_kernel(sink_ref, sep_ref, diagram_ref, elementals_ref, tiles_ref, corr_ref, plain, turned, re_ref, im_ref):
    times = elementals_ref.shape[0]

    def widen(t, carry):
        re, im = elementals_ref[t, 0], elementals_ref[t, 1]
        plain[t] = jnp.concatenate([re, im], 1)
        turned[t] = jnp.concatenate([-im, re], 1)
        return carry

    lax.fori_loop(0, times, widen, 0)
    contract((sink_ref, sep_ref, diagram_ref), plain, turned, tiles_ref, re_ref, im_ref, corr_ref)


def by_gathered_elementals(eigvecs, phase_index, perambulator, tile_sink, tile_sep, tile_diagram):
    cosine, sine = phases(phase_index)
    vecs = lax.all_to_all(eigvecs, AXIS, split_axis=0, concat_axis=1, tiled=True)[0].astype(jnp.float32)
    cosine, sine = cosine[:, None, None], sine[:, None, None]
    first = cosine * vecs[:, 0] - sine * vecs[:, 1]
    second = sine * vecs[:, 0] + cosine * vecs[:, 1]
    right = jnp.stack([jnp.stack([first, second], -2), jnp.stack([second, -first], -2)], -4).astype(jnp.bfloat16)
    value = jnp.einsum("spck,spcol->okl", vecs.astype(jnp.bfloat16), right, preferred_element_type=jnp.float32)
    elemental = value.astype(jnp.bfloat16)[None]
    gathered = lax.all_gather(elemental, AXIS, axis=0, tiled=True)
    times, _, n, _ = gathered.shape
    tiles = perambulator.shape[0]
    smem = pl.BlockSpec(memory_space=pltpu.SMEM)
    vmem = pl.BlockSpec(memory_space=pltpu.VMEM)
    correlator = pl.pallas_call(
        contract_kernel,
        out_shape=jax.ShapeDtypeStruct((2, tiles), jnp.float32),
        in_specs=[smem] * 3 + [vmem] * 2,
        out_specs=vmem,
        scratch_shapes=[
            pltpu.VMEM((times, n, 2 * n), jnp.bfloat16),
            pltpu.VMEM((times, n, 2 * n), jnp.bfloat16),
            pltpu.VMEM((tiles, n), jnp.float32),
            pltpu.VMEM((tiles, n), jnp.float32),
        ],
        compiler_params=pltpu.CompilerParams(vmem_limit_bytes=VMEM_LIMIT),
    )(tile_sink[:, 0], tile_sep, tile_diagram, gathered, widened(perambulator))
    return elemental, correlator.T


def local(eigvecs, *rest):
    devices = lax.axis_size(AXIS)
    small = eigvecs.size * eigvecs.dtype.itemsize * devices <= GATHER_BYTES
    if small and devices & (devices - 1) == 0:
        return by_gathered_vectors(eigvecs, *rest)
    return by_gathered_elementals(eigvecs, *rest)


def solution(mesh):
    return jax.shard_map(
        local,
        mesh=mesh,
        in_specs=(
            P("groups", "space", None, None, None),
            P("groups"),
            P(("groups", "space"), None, None, None),
            P(("groups", "space"), None),
            P(("groups", "space")),
            P(("groups", "space")),
        ),
        out_specs=(P(("groups", "space"), None, None, None), P(("groups", "space"), None)),
        check_vma=False,
    )
```

```python
import functools
import math

import jax
import jax.numpy as jnp
from jax import lax
from jax.experimental import pallas as pl
from jax.experimental.pallas import tpu as pltpu
from jax.sharding import PartitionSpec as P

PERIOD = 48
AXIS = "space"
GATHER_BYTES = 8 << 20
VMEM_LIMIT = 48 << 20


def phases(indices):
    angle = 2.0 * math.pi / PERIOD * indices.astype(jnp.float32)
    return (jnp.cos(angle), jnp.sin(angle))


def swap(block, offset):
    size = lax.axis_size(AXIS)
    return lax.ppermute(block, AXIS, [(i, i ^ offset) for i in range(size)])


def step(held, offset):
    return [(swap(array, offset), tuple(k ^ offset for k in owners)) for array, owners in held]


def stacked(held):
    return jnp.stack([array for array, _ in held], 0), sum((owners for _, owners in held), ())


def swapped(values):
    other = lax.broadcasted_iota(jnp.int32, (8, values.shape[1]), 0) ^ 1
    pieces = [jnp.take_along_axis(values[i : i + 8], other, axis=0) for i in range(0, values.shape[0], 8)]
    return jnp.concatenate(pieces, 0)


def tile_terms(left, right, left_turned, right_turned, tile):
    n = tile.shape[0]
    dot = functools.partial(jnp.dot, preferred_element_type=jnp.float32)
    turned = jnp.concatenate([-tile[:, n:], tile[:, :n]], 1)
    first = dot(left, jnp.concatenate([tile, turned], 0))
    second = dot(tile, jnp.concatenate([right, right_turned], 0))
    fr, fi, sr, si = first[:, :n], first[:, n:], second[:, :n], second[:, n:]
    return (
        jnp.sum(fr * sr + fi * si, axis=0, keepdims=True),
        jnp.sum(fi * sr - fr * si, axis=0, keepdims=True),
    )


def pick(sink_ref, sep_ref, diagram_ref, i, times):
    sink = sink_ref[i]
    source = lax.rem(lax.rem(sink - sep_ref[i], times) + times, times)
    flipped = diagram_ref[i] == 1
    return jnp.where(flipped, source, sink), jnp.where(flipped, sink, source), jnp.where(flipped, -1.0, 1.0)


def contract(ids, plain, turned, tiles_ref, re_ref, im_ref, corr_ref):
    count = tiles_ref.shape[0]

    def one(i, carry):
        a, b, sign = pick(*ids, i, plain.shape[0])
        re, im = tile_terms(plain[a], plain[b], turned[a], turned[b], tiles_ref[i])
        re_ref[pl.ds(i, 1), :] = re
        im_ref[pl.ds(i, 1), :] = im * sign
        return carry

    lax.fori_loop(0, count, one, 0, unroll=math.gcd(count, 16))
    corr_ref[0, :] = jnp.sum(re_ref[...], axis=1)
    corr_ref[1, :] = jnp.sum(im_ref[...], axis=1)


def block_list(refs, pieces):
    loads, owners = [], []
    for ref, piece in zip(refs, pieces):
        for i, k in enumerate(piece):
            loads.append(functools.partial(lambda r, t: r[t], ref if len(piece) == 1 else ref.at[i]))
            owners.append(k)
    return loads, owners


def fill_tables(owners, rows, me, phase_refs, tables):
    n, sites = tables[0].shape[-1], phase_refs[0].shape[1]
    row = lax.broadcasted_iota(jnp.int32, (rows, n), 0)
    sign = jnp.where(row % 2 == 0, -1.0, 1.0)
    for j, k in enumerate(owners):
        for source, plain, signed in zip(phase_refs, tables[:2], tables[2:]):
            line = source[pl.ds(me ^ k, 1), :]
            value = jnp.broadcast_to(line[:, :1], (rows, n))
            for q in range(1, sites):
                value = jnp.where(row >= q * (rows // sites), jnp.broadcast_to(line[:, q : q + 1], (rows, n)), value)
            plain[pl.ds(j * rows, rows)] = value
            signed[pl.ds(j * rows, rows)] = value * sign


def slice_values(loads, t, tables):
    cosine, sine, cosine_signed, sine_signed = tables
    vecs = jnp.concatenate([load(t).astype(jnp.float32) for load in loads], 0)
    other = swapped(vecs)
    first = cosine[...] * vecs + sine_signed[...] * other
    second = sine[...] * vecs - cosine_signed[...] * other
    return lax.dot_general(
        vecs.astype(jnp.bfloat16),
        jnp.concatenate([first.astype(jnp.bfloat16), second.astype(jnp.bfloat16)], 1),
        (((0,), (0,)), ((), ())),
        preferred_element_type=jnp.float32,
    )


def early_kernel(pieces, later, *refs):
    held, refs = refs[: len(pieces)], refs[len(pieces) :]
    cos_ref, sin_ref, sum_ref, later_ref, *tables = refs
    loads, owners = block_list(held, pieces)
    times, rows = sum_ref.shape[0], later_ref.shape[1] // len(later)
    me = lax.axis_index(AXIS).astype(jnp.int32)
    fill_tables(owners, rows, me, (cos_ref, sin_ref), tables)
    fill_tables(later, rows, me, (cos_ref, sin_ref), [later_ref.at[i] for i in range(4)])
    for t in range(times):
        sum_ref[t] = slice_values(loads, t, tables)


def late_kernel(pieces, *refs):
    held, refs = refs[: len(pieces)], refs[len(pieces) :]
    sink_any, sep_any, diagram_any, own_any, tiles_ref, sum_ref, tables_ref, *refs = refs
    elemental_any, corr_ref, plain, turned, re_ref, im_ref, block_ref, out_ref, *ids, sems = refs
    loads_in = [
        pltpu.make_async_copy(source, target, sems.at[i])
        for i, (source, target) in enumerate(zip((own_any, sink_any, sep_any, diagram_any), (block_ref, *ids)))
    ]
    for load in loads_in:
        load.start()
    loads, _ = block_list((block_ref, *held), ((0,), *pieces))
    tables = [tables_ref.at[i] for i in range(4)]
    times, n = plain.shape[:2]
    loads_in[0].wait()
    for t in range(times):
        value = (sum_ref[t] + slice_values(loads, t, tables)).astype(jnp.bfloat16)
        plain[t] = value
        turned[t] = jnp.concatenate([-value[:, n:], value[:, :n]], 1)
    own = plain[lax.axis_index(AXIS).astype(jnp.int32)]
    out_ref[0, 0] = own[:, :n]
    out_ref[0, 1] = own[:, n:]
    store = pltpu.make_async_copy(out_ref, elemental_any, sems.at[4])
    store.start()
    for load in loads_in[1:]:
        load.wait()
    contract(ids, plain, turned, tiles_ref, re_ref, im_ref, corr_ref)
    store.wait()


def widened(perambulator):
    return jnp.concatenate([perambulator[:, 0], perambulator[:, 1]], 2)


def by_gathered_vectors(eigvecs, phase_index, perambulator, tile_sink, tile_sep, tile_diagram):
    times, sites, parts, colors, n = eigvecs.shape
    devices = lax.axis_size(AXIS)
    rows = sites * colors * parts
    block = eigvecs.transpose(0, 1, 3, 2, 4).reshape(times, rows, n)
    own = (block, (0,))
    [far] = step([own], 8)
    [d], [b], [y] = step([own], 6), step([own], 4), step([own], 2)
    [fd], [fb], [fy] = step([far], 6), step([far], 4), step([far], 2)
    near = stacked([far, d, b, y])
    so, sn = step([own, near], 1)
    rest = stacked([fd, fb, fy])
    [sr] = step([rest], 1)
    early, late = [rest, sn, near, so], [sr]
    cosine, sine = (value.reshape(devices, sites) for value in phases(phase_index))
    tiles = perambulator.shape[0]
    vmem = pl.BlockSpec(memory_space=pltpu.VMEM)
    anywhere = pl.BlockSpec(memory_space=pl.ANY)
    early_pieces = [owners for _, owners in early]
    late_pieces = [owners for _, owners in late]
    later = (0, *sum(late_pieces, ()))
    total, tables = pl.pallas_call(
        functools.partial(early_kernel, early_pieces, later),
        out_shape=(
            jax.ShapeDtypeStruct((times, n, 2 * n), jnp.float32),
            jax.ShapeDtypeStruct((4, len(later) * rows, n), jnp.float32),
        ),
        in_specs=[vmem] * (len(early) + 2),
        out_specs=(vmem, vmem),
        scratch_shapes=[pltpu.VMEM((sum(map(len, early_pieces)) * rows, n), jnp.float32)] * 4,
        compiler_params=pltpu.CompilerParams(vmem_limit_bytes=VMEM_LIMIT),
        name="early",
    )(*[array for array, _ in early], cosine, sine)
    elemental, correlator = pl.pallas_call(
        functools.partial(late_kernel, late_pieces),
        out_shape=(
            jax.ShapeDtypeStruct((1, 2, n, n), jnp.bfloat16),
            jax.ShapeDtypeStruct((2, tiles), jnp.float32),
        ),
        in_specs=[vmem] * len(late) + [anywhere] * 4 + [vmem] * 3,
        out_specs=(anywhere, vmem),
        scratch_shapes=[
            pltpu.VMEM((times, n, 2 * n), jnp.bfloat16),
            pltpu.VMEM((times, n, 2 * n), jnp.bfloat16),
            pltpu.VMEM((tiles, n), jnp.float32),
            pltpu.VMEM((tiles, n), jnp.float32),
            pltpu.VMEM(block.shape, block.dtype),
            pltpu.VMEM((1, 2, n, n), jnp.bfloat16),
            *[pltpu.SMEM((tiles,), jnp.int32)] * 3,
            pltpu.SemaphoreType.DMA((5,)),
        ],
        compiler_params=pltpu.CompilerParams(vmem_limit_bytes=VMEM_LIMIT),
        name="late",
    )(*[array for array, _ in late], tile_sink[:, 0], tile_sep, tile_diagram, block, widened(perambulator), total, tables)
    return elemental, correlator.T


def contract_kernel(sink_ref, sep_ref, diagram_ref, elementals_ref, tiles_ref, corr_ref, plain, turned, re_ref, im_ref):
    times = elementals_ref.shape[0]

    def widen(t, carry):
        re, im = elementals_ref[t, 0], elementals_ref[t, 1]
        plain[t] = jnp.concatenate([re, im], 1)
        turned[t] = jnp.concatenate([-im, re], 1)
        return carry

    lax.fori_loop(0, times, widen, 0)
    contract((sink_ref, sep_ref, diagram_ref), plain, turned, tiles_ref, re_ref, im_ref, corr_ref)


def by_gathered_elementals(eigvecs, phase_index, perambulator, tile_sink, tile_sep, tile_diagram):
    cosine, sine = phases(phase_index)
    vecs = lax.all_to_all(eigvecs, AXIS, split_axis=0, concat_axis=1, tiled=True)[0].astype(jnp.float32)
    cosine, sine = cosine[:, None, None], sine[:, None, None]
    first = cosine * vecs[:, 0] - sine * vecs[:, 1]
    second = sine * vecs[:, 0] + cosine * vecs[:, 1]
    right = jnp.stack([jnp.stack([first, second], -2), jnp.stack([second, -first], -2)], -4).astype(jnp.bfloat16)
    value = jnp.einsum("spck,spcol->okl", vecs.astype(jnp.bfloat16), right, preferred_element_type=jnp.float32)
    elemental = value.astype(jnp.bfloat16)[None]
    gathered = lax.all_gather(elemental, AXIS, axis=0, tiled=True)
    times, _, n, _ = gathered.shape
    tiles = perambulator.shape[0]
    smem = pl.BlockSpec(memory_space=pltpu.SMEM)
    vmem = pl.BlockSpec(memory_space=pltpu.VMEM)
    correlator = pl.pallas_call(
        contract_kernel,
        out_shape=jax.ShapeDtypeStruct((2, tiles), jnp.float32),
        in_specs=[smem] * 3 + [vmem] * 2,
        out_specs=vmem,
        scratch_shapes=[
            pltpu.VMEM((times, n, 2 * n), jnp.bfloat16),
            pltpu.VMEM((times, n, 2 * n), jnp.bfloat16),
            pltpu.VMEM((tiles, n), jnp.float32),
            pltpu.VMEM((tiles, n), jnp.float32),
        ],
        compiler_params=pltpu.CompilerParams(vmem_limit_bytes=VMEM_LIMIT),
    )(tile_sink[:, 0], tile_sep, tile_diagram, gathered, widened(perambulator))
    return elemental, correlator.T


def local(eigvecs, *rest):
    devices = lax.axis_size(AXIS)
    small = eigvecs.size * eigvecs.dtype.itemsize * devices <= GATHER_BYTES
    if small and devices & (devices - 1) == 0:
        return by_gathered_vectors(eigvecs, *rest)
    return by_gathered_elementals(eigvecs, *rest)


def solution(mesh):
    return jax.shard_map(
        local,
        mesh=mesh,
        in_specs=(
            P("groups", "space", None, None, None),
            P("groups"),
            P(("groups", "space"), None, None, None),
            P(("groups", "space"), None),
            P(("groups", "space")),
            P(("groups", "space")),
        ),
        out_specs=(P(("groups", "space"), None, None, None), P(("groups", "space"), None)),
        check_vma=False,
    )
```

```python
import functools
import math

import jax
import jax.numpy as jnp
from jax import lax
from jax.experimental import pallas as pl
from jax.experimental.pallas import tpu as pltpu
from jax.sharding import PartitionSpec as P

PERIOD = 48
AXIS = "space"
GATHER_BYTES = 8 << 20
VMEM_LIMIT = 48 << 20


def phases(indices):
    angle = 2.0 * math.pi / PERIOD * indices.astype(jnp.float32)
    return (jnp.cos(angle), jnp.sin(angle))


def swap(block, offset):
    size = lax.axis_size(AXIS)
    return lax.ppermute(block, AXIS, [(i, i ^ offset) for i in range(size)])


def step(held, offset):
    return [(swap(array, offset), tuple(k ^ offset for k in owners)) for array, owners in held]


def stacked(held):
    return jnp.stack([array for array, _ in held], 0), sum((owners for _, owners in held), ())


def swapped(values):
    other = lax.broadcasted_iota(jnp.int32, (8, values.shape[1]), 0) ^ 1
    pieces = [jnp.take_along_axis(values[i : i + 8], other, axis=0) for i in range(0, values.shape[0], 8)]
    return jnp.concatenate(pieces, 0)


def tile_terms(left, right, left_turned, right_turned, tile):
    n = tile.shape[0]
    dot = functools.partial(jnp.dot, preferred_element_type=jnp.float32)
    turned = jnp.concatenate([-tile[:, n:], tile[:, :n]], 1)
    first = dot(left, jnp.concatenate([tile, turned], 0))
    second = dot(tile, jnp.concatenate([right, right_turned], 0))
    fr, fi, sr, si = first[:, :n], first[:, n:], second[:, :n], second[:, n:]
    return (
        jnp.sum(fr * sr + fi * si, axis=0, keepdims=True),
        jnp.sum(fi * sr - fr * si, axis=0, keepdims=True),
    )


def pick(sink_ref, sep_ref, diagram_ref, i, times):
    sink = sink_ref[i]
    source = lax.rem(lax.rem(sink - sep_ref[i], times) + times, times)
    flipped = diagram_ref[i] == 1
    return jnp.where(flipped, source, sink), jnp.where(flipped, sink, source), jnp.where(flipped, -1.0, 1.0)


def contract(ids, plain, turned, tiles_ref, re_ref, im_ref, corr_ref):
    count = tiles_ref.shape[0]

    def one(i, carry):
        a, b, sign = pick(*ids, i, plain.shape[0])
        re, im = tile_terms(plain[a], plain[b], turned[a], turned[b], tiles_ref[i])
        re_ref[pl.ds(i, 1), :] = re
        im_ref[pl.ds(i, 1), :] = im * sign
        return carry

    lax.fori_loop(0, count, one, 0, unroll=math.gcd(count, 16))
    corr_ref[0, :] = jnp.sum(re_ref[...], axis=1)
    corr_ref[1, :] = jnp.sum(im_ref[...], axis=1)


def block_list(refs, pieces):
    loads, owners = [], []
    for ref, piece in zip(refs, pieces):
        for i, k in enumerate(piece):
            loads.append(functools.partial(lambda r, t: r[t], ref if len(piece) == 1 else ref.at[i]))
            owners.append(k)
    return loads, owners


def fill_tables(owners, rows, me, phase_refs, tables):
    n, sites = tables[0].shape[-1], phase_refs[0].shape[1]
    row = lax.broadcasted_iota(jnp.int32, (rows, n), 0)
    sign = jnp.where(row % 2 == 0, -1.0, 1.0)
    for j, k in enumerate(owners):
        for source, plain, signed in zip(phase_refs, tables[:2], tables[2:]):
            line = source[pl.ds(me ^ k, 1), :]
            value = jnp.broadcast_to(line[:, :1], (rows, n))
            for q in range(1, sites):
                value = jnp.where(row >= q * (rows // sites), jnp.broadcast_to(line[:, q : q + 1], (rows, n)), value)
            plain[pl.ds(j * rows, rows)] = value
            signed[pl.ds(j * rows, rows)] = value * sign


def slice_values(loads, t, tables):
    cosine, sine, cosine_signed, sine_signed = tables
    vecs = jnp.concatenate([load(t).astype(jnp.float32) for load in loads], 0)
    other = swapped(vecs)
    first = cosine[...] * vecs + sine_signed[...] * other
    second = sine[...] * vecs - cosine_signed[...] * other
    return lax.dot_general(
        vecs.astype(jnp.bfloat16),
        jnp.concatenate([first.astype(jnp.bfloat16), second.astype(jnp.bfloat16)], 1),
        (((0,), (0,)), ((), ())),
        preferred_element_type=jnp.float32,
    )


def early_kernel(pieces, later, *refs):
    held, refs = refs[: len(pieces)], refs[len(pieces) :]
    cos_ref, sin_ref, sum_ref, later_ref, *tables = refs
    loads, owners = block_list(held, pieces)
    times, rows = sum_ref.shape[0], later_ref.shape[1] // len(later)
    me = lax.axis_index(AXIS).astype(jnp.int32)
    fill_tables(owners, rows, me, (cos_ref, sin_ref), tables)
    fill_tables(later, rows, me, (cos_ref, sin_ref), [later_ref.at[i] for i in range(4)])
    for t in range(times):
        sum_ref[t] = slice_values(loads, t, tables)


def late_kernel(pieces, *refs):
    held, refs = refs[: len(pieces)], refs[len(pieces) :]
    sink_any, sep_any, diagram_any, own_any, tiles_ref, sum_ref, tables_ref, *refs = refs
    elemental_any, corr_ref, plain, turned, re_ref, im_ref, block_ref, out_ref, *ids, sems = refs
    loads_in = [
        pltpu.make_async_copy(source, target, sems.at[i])
        for i, (source, target) in enumerate(zip((own_any, sink_any, sep_any, diagram_any), (block_ref, *ids)))
    ]
    for load in loads_in:
        load.start()
    loads, _ = block_list((block_ref, *held), ((0,), *pieces))
    tables = [tables_ref.at[i] for i in range(4)]
    times, n = plain.shape[:2]
    loads_in[0].wait()
    for t in range(times):
        value = (sum_ref[t] + slice_values(loads, t, tables)).astype(jnp.bfloat16)
        plain[t] = value
        turned[t] = jnp.concatenate([-value[:, n:], value[:, :n]], 1)
    own = plain[lax.axis_index(AXIS).astype(jnp.int32)]
    out_ref[0, 0] = own[:, :n]
    out_ref[0, 1] = own[:, n:]
    store = pltpu.make_async_copy(out_ref, elemental_any, sems.at[4])
    store.start()
    for load in loads_in[1:]:
        load.wait()
    contract(ids, plain, turned, tiles_ref, re_ref, im_ref, corr_ref)
    store.wait()


def widened(perambulator):
    return jnp.concatenate([perambulator[:, 0], perambulator[:, 1]], 2)


def by_gathered_vectors(eigvecs, phase_index, perambulator, tile_sink, tile_sep, tile_diagram):
    times, sites, parts, colors, n = eigvecs.shape
    devices = lax.axis_size(AXIS)
    rows = sites * colors * parts
    block = eigvecs.transpose(0, 1, 3, 2, 4).reshape(times, rows, n)
    own = (block, (0,))
    [far] = step([own], 8)
    [d], [b], [y] = step([own], 6), step([own], 4), step([own], 2)
    [fd], [fb], [fy] = step([far], 6), step([far], 4), step([far], 2)
    [so] = step([own], 1)
    near = stacked([far, y, b, d])
    [sn] = step([near], 1)
    rest = stacked([fd, fb, fy])
    [sr] = step([rest], 1)
    early, late = [rest, sn, near, so], [sr]
    cosine, sine = (value.reshape(devices, sites) for value in phases(phase_index))
    tiles = perambulator.shape[0]
    vmem = pl.BlockSpec(memory_space=pltpu.VMEM)
    anywhere = pl.BlockSpec(memory_space=pl.ANY)
    early_pieces = [owners for _, owners in early]
    late_pieces = [owners for _, owners in late]
    later = (0, *sum(late_pieces, ()))
    total, tables = pl.pallas_call(
        functools.partial(early_kernel, early_pieces, later),
        out_shape=(
            jax.ShapeDtypeStruct((times, n, 2 * n), jnp.float32),
            jax.ShapeDtypeStruct((4, len(later) * rows, n), jnp.float32),
        ),
        in_specs=[vmem] * (len(early) + 2),
        out_specs=(vmem, vmem),
        scratch_shapes=[pltpu.VMEM((sum(map(len, early_pieces)) * rows, n), jnp.float32)] * 4,
        compiler_params=pltpu.CompilerParams(vmem_limit_bytes=VMEM_LIMIT),
        name="early",
    )(*[array for array, _ in early], cosine, sine)
    elemental, correlator = pl.pallas_call(
        functools.partial(late_kernel, late_pieces),
        out_shape=(
            jax.ShapeDtypeStruct((1, 2, n, n), jnp.bfloat16),
            jax.ShapeDtypeStruct((2, tiles), jnp.float32),
        ),
        in_specs=[vmem] * len(late) + [anywhere] * 4 + [vmem] * 3,
        out_specs=(anywhere, vmem),
        scratch_shapes=[
            pltpu.VMEM((times, n, 2 * n), jnp.bfloat16),
            pltpu.VMEM((times, n, 2 * n), jnp.bfloat16),
            pltpu.VMEM((tiles, n), jnp.float32),
            pltpu.VMEM((tiles, n), jnp.float32),
            pltpu.VMEM(block.shape, block.dtype),
            pltpu.VMEM((1, 2, n, n), jnp.bfloat16),
            *[pltpu.SMEM((tiles,), jnp.int32)] * 3,
            pltpu.SemaphoreType.DMA((5,)),
        ],
        compiler_params=pltpu.CompilerParams(vmem_limit_bytes=VMEM_LIMIT),
        name="late",
    )(*[array for array, _ in late], tile_sink[:, 0], tile_sep, tile_diagram, block, widened(perambulator), total, tables)
    return elemental, correlator.T


def contract_kernel(sink_ref, sep_ref, diagram_ref, elementals_ref, tiles_ref, corr_ref, plain, turned, re_ref, im_ref):
    times = elementals_ref.shape[0]

    def widen(t, carry):
        re, im = elementals_ref[t, 0], elementals_ref[t, 1]
        plain[t] = jnp.concatenate([re, im], 1)
        turned[t] = jnp.concatenate([-im, re], 1)
        return carry

    lax.fori_loop(0, times, widen, 0)
    contract((sink_ref, sep_ref, diagram_ref), plain, turned, tiles_ref, re_ref, im_ref, corr_ref)


def by_gathered_elementals(eigvecs, phase_index, perambulator, tile_sink, tile_sep, tile_diagram):
    cosine, sine = phases(phase_index)
    vecs = lax.all_to_all(eigvecs, AXIS, split_axis=0, concat_axis=1, tiled=True)[0].astype(jnp.float32)
    cosine, sine = cosine[:, None, None], sine[:, None, None]
    first = cosine * vecs[:, 0] - sine * vecs[:, 1]
    second = sine * vecs[:, 0] + cosine * vecs[:, 1]
    right = jnp.stack([jnp.stack([first, second], -2), jnp.stack([second, -first], -2)], -4).astype(jnp.bfloat16)
    value = jnp.einsum("spck,spcol->okl", vecs.astype(jnp.bfloat16), right, preferred_element_type=jnp.float32)
    elemental = value.astype(jnp.bfloat16)[None]
    gathered = lax.all_gather(elemental, AXIS, axis=0, tiled=True)
    times, _, n, _ = gathered.shape
    tiles = perambulator.shape[0]
    smem = pl.BlockSpec(memory_space=pltpu.SMEM)
    vmem = pl.BlockSpec(memory_space=pltpu.VMEM)
    correlator = pl.pallas_call(
        contract_kernel,
        out_shape=jax.ShapeDtypeStruct((2, tiles), jnp.float32),
        in_specs=[smem] * 3 + [vmem] * 2,
        out_specs=vmem,
        scratch_shapes=[
            pltpu.VMEM((times, n, 2 * n), jnp.bfloat16),
            pltpu.VMEM((times, n, 2 * n), jnp.bfloat16),
            pltpu.VMEM((tiles, n), jnp.float32),
            pltpu.VMEM((tiles, n), jnp.float32),
        ],
        compiler_params=pltpu.CompilerParams(vmem_limit_bytes=VMEM_LIMIT),
    )(tile_sink[:, 0], tile_sep, tile_diagram, gathered, widened(perambulator))
    return elemental, correlator.T


def local(eigvecs, *rest):
    devices = lax.axis_size(AXIS)
    small = eigvecs.size * eigvecs.dtype.itemsize * devices <= GATHER_BYTES
    if small and devices & (devices - 1) == 0:
        return by_gathered_vectors(eigvecs, *rest)
    return by_gathered_elementals(eigvecs, *rest)


def solution(mesh):
    return jax.shard_map(
        local,
        mesh=mesh,
        in_specs=(
            P("groups", "space", None, None, None),
            P("groups"),
            P(("groups", "space"), None, None, None),
            P(("groups", "space"), None),
            P(("groups", "space")),
            P(("groups", "space")),
        ),
        out_specs=(P(("groups", "space"), None, None, None), P(("groups", "space"), None)),
        check_vma=False,
    )
```

```python
import functools
import math

import jax
import jax.numpy as jnp
from jax import lax
from jax.experimental import pallas as pl
from jax.experimental.pallas import tpu as pltpu
from jax.sharding import PartitionSpec as P

PERIOD = 48
AXIS = "space"
GATHER_BYTES = 8 << 20
VMEM_LIMIT = 48 << 20


def phases(indices):
    angle = 2.0 * math.pi / PERIOD * indices.astype(jnp.float32)
    return (jnp.cos(angle), jnp.sin(angle))


def swap(block, offset):
    size = lax.axis_size(AXIS)
    return lax.ppermute(block, AXIS, [(i, i ^ offset) for i in range(size)])


def step(held, offset):
    return [(swap(array, offset), tuple(k ^ offset for k in owners)) for array, owners in held]


def stacked(held):
    return jnp.stack([array for array, _ in held], 0), sum((owners for _, owners in held), ())


def swapped(values):
    other = lax.broadcasted_iota(jnp.int32, (8, values.shape[1]), 0) ^ 1
    pieces = [jnp.take_along_axis(values[i : i + 8], other, axis=0) for i in range(0, values.shape[0], 8)]
    return jnp.concatenate(pieces, 0)


def tile_terms(left, right, left_turned, right_turned, tile):
    n = tile.shape[0]
    dot = functools.partial(jnp.dot, preferred_element_type=jnp.float32)
    turned = jnp.concatenate([-tile[:, n:], tile[:, :n]], 1)
    first = dot(left, jnp.concatenate([tile, turned], 0))
    second = dot(tile, jnp.concatenate([right, right_turned], 0))
    fr, fi, sr, si = first[:, :n], first[:, n:], second[:, :n], second[:, n:]
    return (
        jnp.sum(fr * sr + fi * si, axis=0, keepdims=True),
        jnp.sum(fi * sr - fr * si, axis=0, keepdims=True),
    )


def pick(sink_ref, sep_ref, diagram_ref, i, times):
    sink = sink_ref[i]
    source = lax.rem(lax.rem(sink - sep_ref[i], times) + times, times)
    flipped = diagram_ref[i] == 1
    return jnp.where(flipped, source, sink), jnp.where(flipped, sink, source), jnp.where(flipped, -1.0, 1.0)


def contract(ids, plain, turned, tiles_ref, re_ref, im_ref, corr_ref):
    count = tiles_ref.shape[0]

    def one(i, carry):
        a, b, sign = pick(*ids, i, plain.shape[0])
        re, im = tile_terms(plain[a], plain[b], turned[a], turned[b], tiles_ref[i])
        re_ref[pl.ds(i, 1), :] = re
        im_ref[pl.ds(i, 1), :] = im * sign
        return carry

    lax.fori_loop(0, count, one, 0, unroll=math.gcd(count, 16))
    corr_ref[0, :] = jnp.sum(re_ref[...], axis=1)
    corr_ref[1, :] = jnp.sum(im_ref[...], axis=1)


def block_list(refs, pieces):
    loads, owners = [], []
    for ref, piece in zip(refs, pieces):
        for i, k in enumerate(piece):
            loads.append(functools.partial(lambda r, t: r[t], ref if len(piece) == 1 else ref.at[i]))
            owners.append(k)
    return loads, owners


def fill_tables(owners, rows, me, phase_refs, tables):
    n, sites = tables[0].shape[-1], phase_refs[0].shape[1]
    row = lax.broadcasted_iota(jnp.int32, (rows, n), 0)
    sign = jnp.where(row % 2 == 0, -1.0, 1.0)
    for j, k in enumerate(owners):
        for source, plain, signed in zip(phase_refs, tables[:2], tables[2:]):
            line = source[pl.ds(me ^ k, 1), :]
            value = jnp.broadcast_to(line[:, :1], (rows, n))
            for q in range(1, sites):
                value = jnp.where(row >= q * (rows // sites), jnp.broadcast_to(line[:, q : q + 1], (rows, n)), value)
            plain[pl.ds(j * rows, rows)] = value
            signed[pl.ds(j * rows, rows)] = value * sign


def slice_values(loads, t, tables):
    cosine, sine, cosine_signed, sine_signed = tables
    vecs = jnp.concatenate([load(t).astype(jnp.float32) for load in loads], 0)
    other = swapped(vecs)
    first = cosine[...] * vecs + sine_signed[...] * other
    second = sine[...] * vecs - cosine_signed[...] * other
    return lax.dot_general(
        vecs.astype(jnp.bfloat16),
        jnp.concatenate([first.astype(jnp.bfloat16), second.astype(jnp.bfloat16)], 1),
        (((0,), (0,)), ((), ())),
        preferred_element_type=jnp.float32,
    )


def early_kernel(pieces, later, *refs):
    held, refs = refs[: len(pieces)], refs[len(pieces) :]
    cos_ref, sin_ref, sum_ref, later_ref, *tables = refs
    loads, owners = block_list(held, pieces)
    times, rows = sum_ref.shape[0], later_ref.shape[1] // len(later)
    me = lax.axis_index(AXIS).astype(jnp.int32)
    fill_tables(owners, rows, me, (cos_ref, sin_ref), tables)
    fill_tables(later, rows, me, (cos_ref, sin_ref), [later_ref.at[i] for i in range(4)])
    for t in range(times):
        sum_ref[t] = slice_values(loads, t, tables)


def late_kernel(pieces, *refs):
    held, refs = refs[: len(pieces)], refs[len(pieces) :]
    sink_any, sep_any, diagram_any, own_any, tiles_ref, sum_ref, tables_ref, *refs = refs
    elemental_any, corr_ref, plain, turned, re_ref, im_ref, block_ref, out_ref, *ids, sems = refs
    loads_in = [
        pltpu.make_async_copy(source, target, sems.at[i])
        for i, (source, target) in enumerate(zip((own_any, sink_any, sep_any, diagram_any), (block_ref, *ids)))
    ]
    for load in loads_in:
        load.start()
    loads, _ = block_list((block_ref, *held), ((0,), *pieces))
    tables = [tables_ref.at[i] for i in range(4)]
    times, n = plain.shape[:2]
    loads_in[0].wait()
    for t in range(times):
        value = (sum_ref[t] + slice_values(loads, t, tables)).astype(jnp.bfloat16)
        plain[t] = value
        turned[t] = jnp.concatenate([-value[:, n:], value[:, :n]], 1)
    own = plain[lax.axis_index(AXIS).astype(jnp.int32)]
    out_ref[0, 0] = own[:, :n]
    out_ref[0, 1] = own[:, n:]
    store = pltpu.make_async_copy(out_ref, elemental_any, sems.at[4])
    store.start()
    for load in loads_in[1:]:
        load.wait()
    contract(ids, plain, turned, tiles_ref, re_ref, im_ref, corr_ref)
    store.wait()


def widened(perambulator):
    return jnp.concatenate([perambulator[:, 0], perambulator[:, 1]], 2)


def by_gathered_vectors(eigvecs, phase_index, perambulator, tile_sink, tile_sep, tile_diagram):
    times, sites, parts, colors, n = eigvecs.shape
    devices = lax.axis_size(AXIS)
    rows = sites * colors * parts
    block = eigvecs.transpose(0, 1, 3, 2, 4).reshape(times, rows, n)
    own = (block, (0,))
    outer, bit = [own], devices // 2
    while bit >= 8:
        outer += step(outer, bit)
        bit //= 2
    far = outer[1:]
    d, b, y = (step([own], offset) for offset in (6, 4, 2))
    far_d, far_b, far_y = (step(far, offset) for offset in (6, 4, 2))
    [side] = step([own], 1)
    near = stacked([*far, *y, *b, *d])
    [side_near] = step([near], 1)
    rest = stacked([*far_d, *far_b, *far_y])
    [side_rest] = step([rest], 1)
    early, late = [rest, near, side_near, side], [side_rest]
    cosine, sine = (value.reshape(devices, sites) for value in phases(phase_index))
    tiles = perambulator.shape[0]
    vmem = pl.BlockSpec(memory_space=pltpu.VMEM)
    anywhere = pl.BlockSpec(memory_space=pl.ANY)
    early_pieces = [owners for _, owners in early]
    late_pieces = [owners for _, owners in late]
    later = (0, *sum(late_pieces, ()))
    total, tables = pl.pallas_call(
        functools.partial(early_kernel, early_pieces, later),
        out_shape=(
            jax.ShapeDtypeStruct((times, n, 2 * n), jnp.float32),
            jax.ShapeDtypeStruct((4, len(later) * rows, n), jnp.float32),
        ),
        in_specs=[vmem] * (len(early) + 2),
        out_specs=(vmem, vmem),
        scratch_shapes=[pltpu.VMEM((sum(map(len, early_pieces)) * rows, n), jnp.float32)] * 4,
        compiler_params=pltpu.CompilerParams(vmem_limit_bytes=VMEM_LIMIT),
        name="early",
    )(*[array for array, _ in early], cosine, sine)
    elemental, correlator = pl.pallas_call(
        functools.partial(late_kernel, late_pieces),
        out_shape=(
            jax.ShapeDtypeStruct((1, 2, n, n), jnp.bfloat16),
            jax.ShapeDtypeStruct((2, tiles), jnp.float32),
        ),
        in_specs=[vmem] * len(late) + [anywhere] * 4 + [vmem] * 3,
        out_specs=(anywhere, vmem),
        scratch_shapes=[
            pltpu.VMEM((times, n, 2 * n), jnp.bfloat16),
            pltpu.VMEM((times, n, 2 * n), jnp.bfloat16),
            pltpu.VMEM((tiles, n), jnp.float32),
            pltpu.VMEM((tiles, n), jnp.float32),
            pltpu.VMEM(block.shape, block.dtype),
            pltpu.VMEM((1, 2, n, n), jnp.bfloat16),
            *[pltpu.SMEM((tiles,), jnp.int32)] * 3,
            pltpu.SemaphoreType.DMA((5,)),
        ],
        compiler_params=pltpu.CompilerParams(vmem_limit_bytes=VMEM_LIMIT),
        name="late",
    )(*[array for array, _ in late], tile_sink[:, 0], tile_sep, tile_diagram, block, widened(perambulator), total, tables)
    return elemental, correlator.T


def contract_kernel(sink_ref, sep_ref, diagram_ref, elementals_ref, tiles_ref, corr_ref, plain, turned, re_ref, im_ref):
    times = elementals_ref.shape[0]

    def widen(t, carry):
        re, im = elementals_ref[t, 0], elementals_ref[t, 1]
        plain[t] = jnp.concatenate([re, im], 1)
        turned[t] = jnp.concatenate([-im, re], 1)
        return carry

    lax.fori_loop(0, times, widen, 0)
    contract((sink_ref, sep_ref, diagram_ref), plain, turned, tiles_ref, re_ref, im_ref, corr_ref)


def by_gathered_elementals(eigvecs, phase_index, perambulator, tile_sink, tile_sep, tile_diagram):
    cosine, sine = phases(phase_index)
    vecs = lax.all_to_all(eigvecs, AXIS, split_axis=0, concat_axis=1, tiled=True)[0].astype(jnp.float32)
    cosine, sine = cosine[:, None, None], sine[:, None, None]
    first = cosine * vecs[:, 0] - sine * vecs[:, 1]
    second = sine * vecs[:, 0] + cosine * vecs[:, 1]
    right = jnp.stack([jnp.stack([first, second], -2), jnp.stack([second, -first], -2)], -4).astype(jnp.bfloat16)
    value = jnp.einsum("spck,spcol->okl", vecs.astype(jnp.bfloat16), right, preferred_element_type=jnp.float32)
    elemental = value.astype(jnp.bfloat16)[None]
    gathered = lax.all_gather(elemental, AXIS, axis=0, tiled=True)
    times, _, n, _ = gathered.shape
    tiles = perambulator.shape[0]
    smem = pl.BlockSpec(memory_space=pltpu.SMEM)
    vmem = pl.BlockSpec(memory_space=pltpu.VMEM)
    correlator = pl.pallas_call(
        contract_kernel,
        out_shape=jax.ShapeDtypeStruct((2, tiles), jnp.float32),
        in_specs=[smem] * 3 + [vmem] * 2,
        out_specs=vmem,
        scratch_shapes=[
            pltpu.VMEM((times, n, 2 * n), jnp.bfloat16),
            pltpu.VMEM((times, n, 2 * n), jnp.bfloat16),
            pltpu.VMEM((tiles, n), jnp.float32),
            pltpu.VMEM((tiles, n), jnp.float32),
        ],
        compiler_params=pltpu.CompilerParams(vmem_limit_bytes=VMEM_LIMIT),
    )(tile_sink[:, 0], tile_sep, tile_diagram, gathered, widened(perambulator))
    return elemental, correlator.T


def local(eigvecs, *rest):
    devices = lax.axis_size(AXIS)
    times, sites, parts, colors, _ = eigvecs.shape
    small = eigvecs.size * eigvecs.dtype.itemsize * devices <= GATHER_BYTES
    paired = devices >= 16 and devices & (devices - 1) == 0
    whole = times == devices and sites * parts * colors % 8 == 0
    if small and paired and whole:
        return by_gathered_vectors(eigvecs, *rest)
    return by_gathered_elementals(eigvecs, *rest)


def solution(mesh):
    return jax.shard_map(
        local,
        mesh=mesh,
        in_specs=(
            P("groups", "space", None, None, None),
            P("groups"),
            P(("groups", "space"), None, None, None),
            P(("groups", "space"), None),
            P(("groups", "space")),
            P(("groups", "space")),
        ),
        out_specs=(P(("groups", "space"), None, None, None), P(("groups", "space"), None)),
        check_vma=False,
    )
```

```python
import functools
import math

import jax
import jax.numpy as jnp
from jax import lax
from jax.experimental import pallas as pl
from jax.experimental.pallas import tpu as pltpu
from jax.sharding import PartitionSpec as P

PERIOD = 48
AXIS = "space"
GATHER_BYTES = 8 << 20
VMEM_LIMIT = 48 << 20


def phases(indices):
    angle = 2.0 * math.pi / PERIOD * indices.astype(jnp.float32)
    return (jnp.cos(angle), jnp.sin(angle))


def swap(block, offset):
    size = lax.axis_size(AXIS)
    return lax.ppermute(block, AXIS, [(i, i ^ offset) for i in range(size)])


def step(held, offset):
    return [(swap(array, offset), tuple(k ^ offset for k in owners)) for array, owners in held]


def stacked(held):
    return jnp.stack([array for array, _ in held], 0), sum((owners for _, owners in held), ())


def swapped(values):
    other = lax.broadcasted_iota(jnp.int32, (8, values.shape[1]), 0) ^ 1
    pieces = [jnp.take_along_axis(values[i : i + 8], other, axis=0) for i in range(0, values.shape[0], 8)]
    return jnp.concatenate(pieces, 0)


def tile_terms(left, right, left_turned, right_turned, tile):
    n = tile.shape[0]
    dot = functools.partial(jnp.dot, preferred_element_type=jnp.float32)
    turned = jnp.concatenate([-tile[:, n:], tile[:, :n]], 1)
    first = dot(left, jnp.concatenate([tile, turned], 0))
    second = dot(tile, jnp.concatenate([right, right_turned], 0))
    fr, fi, sr, si = first[:, :n], first[:, n:], second[:, :n], second[:, n:]
    return (
        jnp.sum(fr * sr + fi * si, axis=0, keepdims=True),
        jnp.sum(fi * sr - fr * si, axis=0, keepdims=True),
    )


def pick(sink_ref, sep_ref, diagram_ref, i, times):
    sink = sink_ref[i]
    source = lax.rem(lax.rem(sink - sep_ref[i], times) + times, times)
    flipped = diagram_ref[i] == 1
    return jnp.where(flipped, source, sink), jnp.where(flipped, sink, source), jnp.where(flipped, -1.0, 1.0)


def contract(ids, plain, turned, tiles_ref, re_ref, im_ref, corr_ref):
    count = tiles_ref.shape[0]

    def one(i, carry):
        a, b, sign = pick(*ids, i, plain.shape[0])
        re, im = tile_terms(plain[a], plain[b], turned[a], turned[b], tiles_ref[i])
        re_ref[pl.ds(i, 1), :] = re
        im_ref[pl.ds(i, 1), :] = im * sign
        return carry

    lax.fori_loop(0, count, one, 0, unroll=math.gcd(count, 16))
    corr_ref[0, :] = jnp.sum(re_ref[...], axis=1)
    corr_ref[1, :] = jnp.sum(im_ref[...], axis=1)


def block_list(refs, pieces):
    loads, owners = [], []
    for ref, piece in zip(refs, pieces):
        for i, k in enumerate(piece):
            loads.append(functools.partial(lambda r, t: r[t], ref if len(piece) == 1 else ref.at[i]))
            owners.append(k)
    return loads, owners


def fill_tables(owners, rows, me, phase_refs, tables):
    n, sites = tables[0].shape[-1], phase_refs[0].shape[1]
    row = lax.broadcasted_iota(jnp.int32, (rows, n), 0)
    sign = jnp.where(row % 2 == 0, -1.0, 1.0)
    for j, k in enumerate(owners):
        for source, plain, signed in zip(phase_refs, tables[:2], tables[2:]):
            line = source[pl.ds(me ^ k, 1), :]
            value = jnp.broadcast_to(line[:, :1], (rows, n))
            for q in range(1, sites):
                value = jnp.where(row >= q * (rows // sites), jnp.broadcast_to(line[:, q : q + 1], (rows, n)), value)
            plain[pl.ds(j * rows, rows)] = value
            signed[pl.ds(j * rows, rows)] = value * sign


def slice_values(loads, t, tables):
    cosine, sine, cosine_signed, sine_signed = tables
    vecs = jnp.concatenate([load(t).astype(jnp.float32) for load in loads], 0)
    other = swapped(vecs)
    first = cosine[...] * vecs + sine_signed[...] * other
    second = sine[...] * vecs - cosine_signed[...] * other
    return lax.dot_general(
        vecs.astype(jnp.bfloat16),
        jnp.concatenate([first.astype(jnp.bfloat16), second.astype(jnp.bfloat16)], 1),
        (((0,), (0,)), ((), ())),
        preferred_element_type=jnp.float32,
    )


def early_kernel(pieces, later, *refs):
    held, refs = refs[: len(pieces)], refs[len(pieces) :]
    cos_ref, sin_ref, sum_ref, later_ref, *tables = refs
    loads, owners = block_list(held, pieces)
    times, rows = sum_ref.shape[0], later_ref.shape[1] // len(later)
    me = lax.axis_index(AXIS).astype(jnp.int32)
    fill_tables(owners, rows, me, (cos_ref, sin_ref), tables)
    fill_tables(later, rows, me, (cos_ref, sin_ref), [later_ref.at[i] for i in range(4)])
    for t in range(times):
        sum_ref[t] = slice_values(loads, t, tables)


def late_kernel(pieces, *refs):
    held, refs = refs[: len(pieces)], refs[len(pieces) :]
    sink_any, sep_any, diagram_any, block_ref, tiles_ref, sum_ref, tables_ref, *refs = refs
    elemental_any, corr_ref, plain, turned, re_ref, im_ref, out_ref, *ids, sems = refs
    loads_in = [
        pltpu.make_async_copy(source, target, sems.at[i])
        for i, (source, target) in enumerate(zip((sink_any, sep_any, diagram_any), ids))
    ]
    for load in loads_in:
        load.start()
    loads, _ = block_list((block_ref, *held), ((0,), *pieces))
    tables = [tables_ref.at[i] for i in range(4)]
    times, n = plain.shape[:2]
    for t in range(times):
        value = (sum_ref[t] + slice_values(loads, t, tables)).astype(jnp.bfloat16)
        plain[t] = value
        turned[t] = jnp.concatenate([-value[:, n:], value[:, :n]], 1)
    own = plain[lax.axis_index(AXIS).astype(jnp.int32)]
    out_ref[0, 0] = own[:, :n]
    out_ref[0, 1] = own[:, n:]
    store = pltpu.make_async_copy(out_ref, elemental_any, sems.at[3])
    store.start()
    for load in loads_in:
        load.wait()
    contract(ids, plain, turned, tiles_ref, re_ref, im_ref, corr_ref)
    store.wait()


def widened(perambulator):
    return jnp.concatenate([perambulator[:, 0], perambulator[:, 1]], 2)


def by_gathered_vectors(eigvecs, phase_index, perambulator, tile_sink, tile_sep, tile_diagram):
    times, sites, parts, colors, n = eigvecs.shape
    devices = lax.axis_size(AXIS)
    rows = sites * colors * parts
    block = eigvecs.transpose(0, 1, 3, 2, 4).reshape(times, rows, n)
    own = (block, (0,))
    outer, bit = [own], devices // 2
    while bit >= 8:
        outer += step(outer, bit)
        bit //= 2
    far = outer[1:]
    d, b, y = (step([own], offset) for offset in (6, 4, 2))
    far_d, far_b, far_y = (step(far, offset) for offset in (6, 4, 2))
    [side] = step([own], 1)
    near = stacked([*far, *y, *b, *d])
    [side_near] = step([near], 1)
    rest = stacked([*far_d, *far_b, *far_y])
    [side_rest] = step([rest], 1)
    early, late = [rest, near, side_near, side], [side_rest]
    cosine, sine = (value.reshape(devices, sites) for value in phases(phase_index))
    tiles = perambulator.shape[0]
    vmem = pl.BlockSpec(memory_space=pltpu.VMEM)
    anywhere = pl.BlockSpec(memory_space=pl.ANY)
    early_pieces = [owners for _, owners in early]
    late_pieces = [owners for _, owners in late]
    later = (0, *sum(late_pieces, ()))
    total, tables = pl.pallas_call(
        functools.partial(early_kernel, early_pieces, later),
        out_shape=(
            jax.ShapeDtypeStruct((times, n, 2 * n), jnp.float32),
            jax.ShapeDtypeStruct((4, len(later) * rows, n), jnp.float32),
        ),
        in_specs=[vmem] * (len(early) + 2),
        out_specs=(vmem, vmem),
        scratch_shapes=[pltpu.VMEM((sum(map(len, early_pieces)) * rows, n), jnp.float32)] * 4,
        compiler_params=pltpu.CompilerParams(vmem_limit_bytes=VMEM_LIMIT),
        name="early",
    )(*[array for array, _ in early], cosine, sine)
    elemental, correlator = pl.pallas_call(
        functools.partial(late_kernel, late_pieces),
        out_shape=(
            jax.ShapeDtypeStruct((1, 2, n, n), jnp.bfloat16),
            jax.ShapeDtypeStruct((2, tiles), jnp.float32),
        ),
        in_specs=[vmem] * len(late) + [anywhere] * 3 + [vmem] * 4,
        out_specs=(anywhere, vmem),
        scratch_shapes=[
            pltpu.VMEM((times, n, 2 * n), jnp.bfloat16),
            pltpu.VMEM((times, n, 2 * n), jnp.bfloat16),
            pltpu.VMEM((tiles, n), jnp.float32),
            pltpu.VMEM((tiles, n), jnp.float32),
            pltpu.VMEM((1, 2, n, n), jnp.bfloat16),
            *[pltpu.SMEM((tiles,), jnp.int32)] * 3,
            pltpu.SemaphoreType.DMA((4,)),
        ],
        compiler_params=pltpu.CompilerParams(vmem_limit_bytes=VMEM_LIMIT),
        name="late",
    )(*[array for array, _ in late], tile_sink[:, 0], tile_sep, tile_diagram, block, widened(perambulator), total, tables)
    return elemental, correlator.T


def contract_kernel(sink_ref, sep_ref, diagram_ref, elementals_ref, tiles_ref, corr_ref, plain, turned, re_ref, im_ref):
    times = elementals_ref.shape[0]

    def widen(t, carry):
        re, im = elementals_ref[t, 0], elementals_ref[t, 1]
        plain[t] = jnp.concatenate([re, im], 1)
        turned[t] = jnp.concatenate([-im, re], 1)
        return carry

    lax.fori_loop(0, times, widen, 0)
    contract((sink_ref, sep_ref, diagram_ref), plain, turned, tiles_ref, re_ref, im_ref, corr_ref)


def by_gathered_elementals(eigvecs, phase_index, perambulator, tile_sink, tile_sep, tile_diagram):
    cosine, sine = phases(phase_index)
    vecs = lax.all_to_all(eigvecs, AXIS, split_axis=0, concat_axis=1, tiled=True)[0].astype(jnp.float32)
    cosine, sine = cosine[:, None, None], sine[:, None, None]
    first = cosine * vecs[:, 0] - sine * vecs[:, 1]
    second = sine * vecs[:, 0] + cosine * vecs[:, 1]
    right = jnp.stack([jnp.stack([first, second], -2), jnp.stack([second, -first], -2)], -4).astype(jnp.bfloat16)
    value = jnp.einsum("spck,spcol->okl", vecs.astype(jnp.bfloat16), right, preferred_element_type=jnp.float32)
    elemental = value.astype(jnp.bfloat16)[None]
    gathered = lax.all_gather(elemental, AXIS, axis=0, tiled=True)
    times, _, n, _ = gathered.shape
    tiles = perambulator.shape[0]
    smem = pl.BlockSpec(memory_space=pltpu.SMEM)
    vmem = pl.BlockSpec(memory_space=pltpu.VMEM)
    correlator = pl.pallas_call(
        contract_kernel,
        out_shape=jax.ShapeDtypeStruct((2, tiles), jnp.float32),
        in_specs=[smem] * 3 + [vmem] * 2,
        out_specs=vmem,
        scratch_shapes=[
            pltpu.VMEM((times, n, 2 * n), jnp.bfloat16),
            pltpu.VMEM((times, n, 2 * n), jnp.bfloat16),
            pltpu.VMEM((tiles, n), jnp.float32),
            pltpu.VMEM((tiles, n), jnp.float32),
        ],
        compiler_params=pltpu.CompilerParams(vmem_limit_bytes=VMEM_LIMIT),
    )(tile_sink[:, 0], tile_sep, tile_diagram, gathered, widened(perambulator))
    return elemental, correlator.T


def local(eigvecs, *rest):
    devices = lax.axis_size(AXIS)
    times, sites, parts, colors, _ = eigvecs.shape
    small = eigvecs.size * eigvecs.dtype.itemsize * devices <= GATHER_BYTES
    paired = devices >= 16 and devices & (devices - 1) == 0
    whole = times == devices and sites * parts * colors % 8 == 0
    if small and paired and whole:
        return by_gathered_vectors(eigvecs, *rest)
    return by_gathered_elementals(eigvecs, *rest)


def solution(mesh):
    return jax.shard_map(
        local,
        mesh=mesh,
        in_specs=(
            P("groups", "space", None, None, None),
            P("groups"),
            P(("groups", "space"), None, None, None),
            P(("groups", "space"), None),
            P(("groups", "space")),
            P(("groups", "space")),
        ),
        out_specs=(P(("groups", "space"), None, None, None), P(("groups", "space"), None)),
        check_vma=False,
    )
```

```python
import functools
import math

import jax
import jax.numpy as jnp
from jax import lax
from jax.experimental import pallas as pl
from jax.experimental.pallas import tpu as pltpu
from jax.sharding import PartitionSpec as P

PERIOD = 48
AXIS = "space"
GATHER_BYTES = 8 << 20
VMEM_LIMIT = 48 << 20


def phases(indices):
    angle = 2.0 * math.pi / PERIOD * indices.astype(jnp.float32)
    return (jnp.cos(angle), jnp.sin(angle))


def swap(block, offset):
    size = lax.axis_size(AXIS)
    return lax.ppermute(block, AXIS, [(i, i ^ offset) for i in range(size)])


def step(held, offset):
    return [(swap(array, offset), tuple(k ^ offset for k in owners)) for array, owners in held]


def stacked(held):
    return jnp.stack([array for array, _ in held], 0), sum((owners for _, owners in held), ())


def swapped(values):
    other = lax.broadcasted_iota(jnp.int32, (8, values.shape[1]), 0) ^ 1
    pieces = [jnp.take_along_axis(values[i : i + 8], other, axis=0) for i in range(0, values.shape[0], 8)]
    return jnp.concatenate(pieces, 0)


def tile_terms(left, right, left_turned, right_turned, tile):
    n = tile.shape[0]
    dot = functools.partial(jnp.dot, preferred_element_type=jnp.float32)
    turned = jnp.concatenate([-tile[:, n:], tile[:, :n]], 1)
    first = dot(left, jnp.concatenate([tile, turned], 0))
    second = dot(tile, jnp.concatenate([right, right_turned], 0))
    fr, fi, sr, si = first[:, :n], first[:, n:], second[:, :n], second[:, n:]
    return (
        jnp.sum(fr * sr + fi * si, axis=0, keepdims=True),
        jnp.sum(fi * sr - fr * si, axis=0, keepdims=True),
    )


def pick(sink_ref, sep_ref, diagram_ref, i, times):
    sink = sink_ref[i]
    source = lax.rem(lax.rem(sink - sep_ref[i], times) + times, times)
    flipped = diagram_ref[i] == 1
    return jnp.where(flipped, source, sink), jnp.where(flipped, sink, source), jnp.where(flipped, -1.0, 1.0)


def contract(ids, plain, turned, tiles, re_ref, im_ref, corr_ref):
    count = tiles[0].shape[0]

    def one(i, carry):
        a, b, sign = pick(*ids, i, plain.shape[0])
        re, im = tile_terms(plain[a], plain[b], turned[a], turned[b], jnp.concatenate([tiles[0][i], tiles[1][i]], 1))
        re_ref[pl.ds(i, 1), :] = re
        im_ref[pl.ds(i, 1), :] = im * sign
        return carry

    lax.fori_loop(0, count, one, 0, unroll=math.gcd(count, 16))
    corr_ref[0, :] = jnp.sum(re_ref[...], axis=1)
    corr_ref[1, :] = jnp.sum(im_ref[...], axis=1)


def block_list(refs, pieces):
    loads, owners = [], []
    for ref, piece in zip(refs, pieces):
        for i, k in enumerate(piece):
            loads.append(functools.partial(lambda r, t: r[t], ref if len(piece) == 1 else ref.at[i]))
            owners.append(k)
    return loads, owners


def fill_tables(owners, rows, me, phase_refs, tables):
    n, sites = tables[0].shape[-1], phase_refs[0].shape[1]
    row = lax.broadcasted_iota(jnp.int32, (rows, n), 0)
    sign = jnp.where(row % 2 == 0, -1.0, 1.0)
    for j, k in enumerate(owners):
        for source, plain, signed in zip(phase_refs, tables[:2], tables[2:]):
            line = source[pl.ds(me ^ k, 1), :]
            value = jnp.broadcast_to(line[:, :1], (rows, n))
            for q in range(1, sites):
                value = jnp.where(row >= q * (rows // sites), jnp.broadcast_to(line[:, q : q + 1], (rows, n)), value)
            plain[pl.ds(j * rows, rows)] = value
            signed[pl.ds(j * rows, rows)] = value * sign


def slice_values(loads, t, tables):
    cosine, sine, cosine_signed, sine_signed = tables
    vecs = jnp.concatenate([load(t).astype(jnp.float32) for load in loads], 0)
    other = swapped(vecs)
    first = cosine[...] * vecs + sine_signed[...] * other
    second = sine[...] * vecs - cosine_signed[...] * other
    return lax.dot_general(
        vecs.astype(jnp.bfloat16),
        jnp.concatenate([first.astype(jnp.bfloat16), second.astype(jnp.bfloat16)], 1),
        (((0,), (0,)), ((), ())),
        preferred_element_type=jnp.float32,
    )


def early_kernel(pieces, later, *refs):
    held, refs = refs[: len(pieces)], refs[len(pieces) :]
    cos_ref, sin_ref, sum_ref, later_ref, *tables = refs
    loads, owners = block_list(held, pieces)
    times, rows = sum_ref.shape[0], later_ref.shape[1] // len(later)
    me = lax.axis_index(AXIS).astype(jnp.int32)
    fill_tables(owners, rows, me, (cos_ref, sin_ref), tables)
    fill_tables(later, rows, me, (cos_ref, sin_ref), [later_ref.at[i] for i in range(4)])
    for t in range(times):
        sum_ref[t] = slice_values(loads, t, tables)


def late_kernel(pieces, *refs):
    held, refs = refs[: len(pieces)], refs[len(pieces) :]
    sink_any, sep_any, diagram_any, own_any, *tiles, sum_ref, tables_ref = refs[:8]
    refs = refs[8:]
    elemental_any, corr_ref, plain, turned, re_ref, im_ref, block_ref, out_ref, *ids, sems = refs
    loads_in = [
        pltpu.make_async_copy(source, target, sems.at[i])
        for i, (source, target) in enumerate(zip((own_any, sink_any, sep_any, diagram_any), (block_ref, *ids)))
    ]
    for load in loads_in:
        load.start()
    loads, _ = block_list((block_ref, *held), ((0,), *pieces))
    tables = [tables_ref.at[i] for i in range(4)]
    times, n = plain.shape[:2]
    loads_in[0].wait()
    for t in range(times):
        value = (sum_ref[t] + slice_values(loads, t, tables)).astype(jnp.bfloat16)
        plain[t] = value
        turned[t] = jnp.concatenate([-value[:, n:], value[:, :n]], 1)
    own = plain[lax.axis_index(AXIS).astype(jnp.int32)]
    out_ref[0, 0] = own[:, :n]
    out_ref[0, 1] = own[:, n:]
    store = pltpu.make_async_copy(out_ref, elemental_any, sems.at[4])
    store.start()
    for load in loads_in[1:]:
        load.wait()
    contract(ids, plain, turned, tiles, re_ref, im_ref, corr_ref)
    store.wait()


def halves(perambulator):
    return perambulator[:, 0], perambulator[:, 1]


def by_gathered_vectors(eigvecs, phase_index, perambulator, tile_sink, tile_sep, tile_diagram):
    times, sites, parts, colors, n = eigvecs.shape
    devices = lax.axis_size(AXIS)
    rows = sites * colors * parts
    block = eigvecs.transpose(0, 1, 3, 2, 4).reshape(times, rows, n)
    own = (block, (0,))
    outer, bit = [own], devices // 2
    while bit >= 8:
        outer += step(outer, bit)
        bit //= 2
    far = outer[1:]
    d, b, y = (step([own], offset) for offset in (6, 4, 2))
    far_d, far_b, far_y = (step(far, offset) for offset in (6, 4, 2))
    [side] = step([own], 1)
    near = stacked([*far, *y, *b, *d])
    [side_near] = step([near], 1)
    rest = stacked([*far_d, *far_b, *far_y])
    [side_rest] = step([rest], 1)
    early, late = [rest, near, side_near, side], [side_rest]
    cosine, sine = (value.reshape(devices, sites) for value in phases(phase_index))
    tiles = perambulator.shape[0]
    vmem = pl.BlockSpec(memory_space=pltpu.VMEM)
    anywhere = pl.BlockSpec(memory_space=pl.ANY)
    early_pieces = [owners for _, owners in early]
    late_pieces = [owners for _, owners in late]
    later = (0, *sum(late_pieces, ()))
    total, tables = pl.pallas_call(
        functools.partial(early_kernel, early_pieces, later),
        out_shape=(
            jax.ShapeDtypeStruct((times, n, 2 * n), jnp.float32),
            jax.ShapeDtypeStruct((4, len(later) * rows, n), jnp.float32),
        ),
        in_specs=[vmem] * (len(early) + 2),
        out_specs=(vmem, vmem),
        scratch_shapes=[pltpu.VMEM((sum(map(len, early_pieces)) * rows, n), jnp.float32)] * 4,
        compiler_params=pltpu.CompilerParams(vmem_limit_bytes=VMEM_LIMIT),
        name="early",
    )(*[array for array, _ in early], cosine, sine)
    elemental, correlator = pl.pallas_call(
        functools.partial(late_kernel, late_pieces),
        out_shape=(
            jax.ShapeDtypeStruct((1, 2, n, n), jnp.bfloat16),
            jax.ShapeDtypeStruct((2, tiles), jnp.float32),
        ),
        in_specs=[vmem] * len(late) + [anywhere] * 4 + [vmem] * 4,
        out_specs=(anywhere, vmem),
        scratch_shapes=[
            pltpu.VMEM((times, n, 2 * n), jnp.bfloat16),
            pltpu.VMEM((times, n, 2 * n), jnp.bfloat16),
            pltpu.VMEM((tiles, n), jnp.float32),
            pltpu.VMEM((tiles, n), jnp.float32),
            pltpu.VMEM(block.shape, block.dtype),
            pltpu.VMEM((1, 2, n, n), jnp.bfloat16),
            *[pltpu.SMEM((tiles,), jnp.int32)] * 3,
            pltpu.SemaphoreType.DMA((5,)),
        ],
        compiler_params=pltpu.CompilerParams(vmem_limit_bytes=VMEM_LIMIT),
        name="late",
    )(*[array for array, _ in late], tile_sink[:, 0], tile_sep, tile_diagram, block, *halves(perambulator), total, tables)
    return elemental, correlator.T


def contract_kernel(sink_ref, sep_ref, diagram_ref, elementals_ref, re_tiles, im_tiles, corr_ref, plain, turned, re_ref, im_ref):
    times = elementals_ref.shape[0]

    def widen(t, carry):
        re, im = elementals_ref[t, 0], elementals_ref[t, 1]
        plain[t] = jnp.concatenate([re, im], 1)
        turned[t] = jnp.concatenate([-im, re], 1)
        return carry

    lax.fori_loop(0, times, widen, 0)
    contract((sink_ref, sep_ref, diagram_ref), plain, turned, (re_tiles, im_tiles), re_ref, im_ref, corr_ref)


def by_gathered_elementals(eigvecs, phase_index, perambulator, tile_sink, tile_sep, tile_diagram):
    cosine, sine = phases(phase_index)
    vecs = lax.all_to_all(eigvecs, AXIS, split_axis=0, concat_axis=1, tiled=True)[0].astype(jnp.float32)
    cosine, sine = cosine[:, None, None], sine[:, None, None]
    first = cosine * vecs[:, 0] - sine * vecs[:, 1]
    second = sine * vecs[:, 0] + cosine * vecs[:, 1]
    right = jnp.stack([jnp.stack([first, second], -2), jnp.stack([second, -first], -2)], -4).astype(jnp.bfloat16)
    value = jnp.einsum("spck,spcol->okl", vecs.astype(jnp.bfloat16), right, preferred_element_type=jnp.float32)
    elemental = value.astype(jnp.bfloat16)[None]
    gathered = lax.all_gather(elemental, AXIS, axis=0, tiled=True)
    times, _, n, _ = gathered.shape
    tiles = perambulator.shape[0]
    smem = pl.BlockSpec(memory_space=pltpu.SMEM)
    vmem = pl.BlockSpec(memory_space=pltpu.VMEM)
    correlator = pl.pallas_call(
        contract_kernel,
        out_shape=jax.ShapeDtypeStruct((2, tiles), jnp.float32),
        in_specs=[smem] * 3 + [vmem] * 3,
        out_specs=vmem,
        scratch_shapes=[
            pltpu.VMEM((times, n, 2 * n), jnp.bfloat16),
            pltpu.VMEM((times, n, 2 * n), jnp.bfloat16),
            pltpu.VMEM((tiles, n), jnp.float32),
            pltpu.VMEM((tiles, n), jnp.float32),
        ],
        compiler_params=pltpu.CompilerParams(vmem_limit_bytes=VMEM_LIMIT),
    )(tile_sink[:, 0], tile_sep, tile_diagram, gathered, *halves(perambulator))
    return elemental, correlator.T


def local(eigvecs, *rest):
    devices = lax.axis_size(AXIS)
    times, sites, parts, colors, _ = eigvecs.shape
    small = eigvecs.size * eigvecs.dtype.itemsize * devices <= GATHER_BYTES
    paired = devices >= 16 and devices & (devices - 1) == 0
    whole = times == devices and sites * parts * colors % 8 == 0
    if small and paired and whole:
        return by_gathered_vectors(eigvecs, *rest)
    return by_gathered_elementals(eigvecs, *rest)


def solution(mesh):
    return jax.shard_map(
        local,
        mesh=mesh,
        in_specs=(
            P("groups", "space", None, None, None),
            P("groups"),
            P(("groups", "space"), None, None, None),
            P(("groups", "space"), None),
            P(("groups", "space")),
            P(("groups", "space")),
        ),
        out_specs=(P(("groups", "space"), None, None, None), P(("groups", "space"), None)),
        check_vma=False,
    )
```
